32 devices in a mesh: groups: 2 (over x), section: 16 (over z, y, core).
Axes of the slice: x: 2, y: 2, z: 4, core: 2. Of those that a mesh axis runs over, the one named last changes fastest.
Arguments:
- arriving: bfloat16 [4096, 4096], P(('groups', 'section')), parts along dimension 0, may hold values from -6 to 6
- memory: bfloat16 [2048, 4096], P(('groups', 'section')), parts along dimension 0, may hold values from -6 to 6
- w_query: bfloat16 [4096, 4096], P(None, 'section'), may hold values from -8 to 8, as said below
- w_key: bfloat16 [4096, 4096], P(None, 'section'), may hold values from -0.09375 to 0.09375
- w_value: bfloat16 [4096, 4096], P(None, 'section'), may hold values from -0.09375 to 0.09375
- w_out: bfloat16 [4096, 4096], P('section'), may hold values from -0.125 to 0.125
- tok_len: int32 [64], P('groups'), parts along dimension 0, may hold values from 16 to 64, as said below
- mem_len: int32 [32], P('groups'), parts along dimension 0, may hold values from 16 to 64, as said below
Outputs:
- mixed: bfloat16 [4096, 4096], P(('groups', 'section')), parts along dimension 0
The draws below stay inside these ranges and needn't reach their ends.
There are 2 independent parts, one for each index of `groups`. The reference program is written for one: setup_inputs(seed, part) draws one part's arguments, and reference() takes and returns one part's arrays. A program takes and returns all parts, laid end to end along the dimension named above; an argument that names none is the same for every part. Nothing has to cross between parts.
Inputs may be any that keep to these rules, and one draw needn't show every extreme that they name: Rows of section s's microbatch b at positions tok_len[s * 16 + b] or later are padding. Frames of utterance u at positions mem_len[u] or later are padding. `w_query`: query projection weights, every entry within the stated range.
All inputs are finite; a program needn't handle non-finite values.
Results may differ from the reference program's by a relative error of at most 0.0028.
The reference program's roundings to bfloat16 on the way count: a program that leaves them out, or rounds other values in their place, can miss the bound.
Values may be sent and summed in bfloat16 or wider, within the bound.
No kernel may reach another device: no remote copies, remote signals or barrier semaphores. Data moves between devices by JAX's collectives and lax.ppermute only.
A program may use at most 128 MiB of HBM per device.

```python
import math
import jax
import jax.numpy as jnp
from jax import lax

D = 4096
HEADS = 16
HD = 128
FR = 64
MB = 16
MEMF = 64
CYCLE = 2
ROWS = 2048
MEMROWS = 1024


def pinned_lengths(key, amount, lowest, highest, pin_low):
    key_one, key_two = jax.random.split(key)
    values_drawn = jax.random.randint(key_one, (amount,), lowest, highest + 1, dtype=jnp.int32)
    shuffle = jax.random.permutation(key_two, amount)
    values_drawn = values_drawn.at[shuffle[0]].set(highest)
    if pin_low:
        values_drawn = values_drawn.at[shuffle[1]].set(lowest)
    return values_drawn


def draw_tok_len(key, part):
    return pinned_lengths(jax.random.fold_in(key, 11), CYCLE * MB, FR // 4, FR, True)


def draw_mem_len(key, part):
    return pinned_lengths(jax.random.fold_in(key, 12), MB, MEMF // 4, MEMF, False)


def draw_w_query(key, part):
    key_one = jax.random.fold_in(jax.random.fold_in(key, 13), 0)
    columns = CYCLE * HEADS * HD
    values_drawn = jax.random.normal(key_one, (D, columns), jnp.float32) * (1.5 / math.sqrt(D))
    return jnp.clip(values_drawn, -8.0, 8.0).astype(jnp.bfloat16)


def block_scale(stream_key, dims, shards, smallest, high):
    factor_of, own = 1.0, jax.random.fold_in(stream_key, 6)
    for axis_at, parts in shards:
        heights = jnp.exp(jax.random.uniform(jax.random.fold_in(own, axis_at), (parts,), jnp.float32, smallest / len(shards), high / len(shards)))
        factor_of = factor_of * jnp.repeat(heights, dims[axis_at] // parts).reshape([-1 if axis == axis_at else 1 for axis in range(len(dims))])
    return factor_of


def noise(stream_key, shape, deviation, reach, pieces=(), kind=jnp.bfloat16):
    gain = block_scale(stream_key, shape, pieces, -0.22, 0.18) if pieces else 1.0
    drawn = jax.random.normal(stream_key, shape, jnp.float32) * deviation * gain
    return jnp.minimum(jnp.maximum(drawn, -reach), reach).astype(kind)


def setup_inputs(seed: int = 0, part: int = 0) -> dict:
    arg_keys = jax.random.split(jax.random.key(seed), 9)
    part_keys = jax.random.split(jax.random.fold_in(arg_keys[8], part), 9)
    arriving = noise(part_keys[0], (ROWS, D), 1.0, 6.0, ((0, 16),))
    memory = noise(part_keys[1], (MEMROWS, D), 1.0, 6.0, ((0, 16),))
    w_query = draw_w_query(jax.random.fold_in(arg_keys[8], 71), part)
    w_key = noise(arg_keys[3], (D, CYCLE * HEADS * HD), D ** -0.5, 0.09375, ((1, 16),))
    w_value = noise(arg_keys[4], (D, CYCLE * HEADS * HD), D ** -0.5, 0.09375, ((1, 16),))
    w_out = noise(arg_keys[5], (CYCLE * HEADS * HD, D), (HEADS * HD) ** -0.5, 0.125, ((0, 16),))
    tok_len = draw_tok_len(jax.random.fold_in(jax.random.fold_in(arg_keys[8], part), 71), part)
    mem_len = draw_mem_len(jax.random.fold_in(jax.random.fold_in(arg_keys[8], part), 71), part)
    return {"arriving": arriving, "memory": memory, "w_query": w_query, "w_key": w_key, "w_value": w_value, "w_out": w_out, "tok_len": tok_len, "mem_len": mem_len}


norm_eps = 1e-06

def reference(arriving, memory, w_query, w_key, w_value, w_out, tok_len, mem_len):
    section_rows = MB * FR
    head_cols = HEADS * HD
    att_scale = 1.0 / math.sqrt(HD)
    results = []
    for section_no in range(CYCLE):
        before = (section_no - 1) % CYCLE
        incoming = arriving[before * section_rows:(before + 1) * section_rows]
        widened = incoming.astype(jnp.float32)
        normed = (widened * lax.rsqrt(lax.optimization_barrier(jnp.mean(widened * widened, -1, keepdims=True)) + norm_eps)).astype(jnp.bfloat16)
        col_low = section_no * head_cols
        queries = jnp.dot(normed, w_query[:, col_low:col_low + head_cols], preferred_element_type=jnp.float32).astype(jnp.bfloat16)
        key_rows = jnp.dot(memory, w_key[:, col_low:col_low + head_cols], preferred_element_type=jnp.float32).astype(jnp.bfloat16)
        val_rows = jnp.dot(memory, w_value[:, col_low:col_low + head_cols], preferred_element_type=jnp.float32).astype(jnp.bfloat16)
        utt_order = (section_no + jnp.arange(MB, dtype=jnp.int32)) % MB
        key_rows = jnp.take(key_rows.reshape(MB, MEMF, HEADS, HD), utt_order, axis=0)
        val_rows = jnp.take(val_rows.reshape(MB, MEMF, HEADS, HD), utt_order, axis=0)
        queries = queries.reshape(MB, FR, HEADS, HD)
        scores = jnp.einsum('bqhd,bkhd->bhqk', queries.astype(jnp.float32), key_rows.astype(jnp.float32)) * att_scale
        lengths = jnp.take(mem_len, utt_order)
        valid = jnp.arange(MEMF, dtype=jnp.int32)[None, :] < lengths[:, None]
        scores = jnp.where(valid[:, None, None, :], scores, -jnp.inf)
        row_max = lax.optimization_barrier(jnp.max(scores, -1, keepdims=True))
        expo = jnp.exp(scores - row_max)
        att_probs = (expo / lax.optimization_barrier(jnp.sum(expo, -1, keepdims=True))).astype(jnp.bfloat16)
        attended = jnp.einsum('bhqk,bkhd->bqhd', att_probs.astype(jnp.float32), val_rows.astype(jnp.float32)).astype(jnp.bfloat16)
        branch = jnp.dot(attended.reshape(section_rows, head_cols), w_out[col_low:col_low + head_cols], preferred_element_type=jnp.float32)
        limits = tok_len[section_no * MB:(section_no + 1) * MB]
        is_live = (jnp.arange(FR, dtype=jnp.int32)[None, :] < limits[:, None]).reshape(section_rows)
        results.append((widened + jnp.where(is_live[:, None], branch, 0.0)).astype(jnp.bfloat16))
    return jnp.concatenate(results, 0)
```

```python
import functools
import math

import jax
import jax.numpy as jnp
from jax import lax
from jax.experimental import pallas as pl
from jax.experimental.pallas import tpu as pltpu
from jax.sharding import PartitionSpec as P

HD = 128
FR = 64
GROUP = 8
MB = 16
MEMF = 64
NORM_EPS = 1e-06
BF16 = jnp.bfloat16
F32 = jnp.float32
VMEM_BYTES = 48 * 2**20

CORE, NEAR, FAR = 1, 2, 4
CHIPS = (0, NEAR, FAR, NEAR | FAR)


def flip(value, bits):
    size = lax.axis_size("section")
    return lax.ppermute(value, "section", [(i, i ^ bits) for i in range(size)])


def hop(value):
    size = lax.axis_size("section")
    return lax.ppermute(value, "section", [(i, (i + GROUP) % size) for i in range(size)])


def across(value):
    return lax.ppermute(value, "groups", [(0, 1), (1, 0)])


def whole(count):
    return [pl.BlockSpec(memory_space=pltpu.VMEM)] * count


def dot(a, b):
    return jnp.dot(a, b, preferred_element_type=F32)


def keys_values_kernel(*refs):
    *mem_refs, key_own, key_oth, val_own, val_oth, out, rows = refs
    for k, ref in enumerate(mem_refs):
        rows[k * MEMF:(k + 1) * MEMF, :] = ref[...]
    width = key_own.shape[1]
    for k, weight in enumerate((key_own, key_oth, val_own, val_oth)):
        out[:, k * width:(k + 1) * width] = dot(rows[...], weight[...]).astype(BF16)


def keys_values(pieces, weights):
    depth, width = weights[0].shape
    rows = len(pieces) * MEMF
    return pl.pallas_call(
        keys_values_kernel,
        out_shape=jax.ShapeDtypeStruct((rows, 4 * width), BF16),
        in_specs=whole(len(pieces) + 4),
        out_specs=pl.BlockSpec(memory_space=pltpu.VMEM),
        scratch_shapes=[pltpu.VMEM((rows, depth), BF16)],
        compiler_params=pltpu.CompilerParams(vmem_limit_bytes=VMEM_BYTES),
        cost_estimate=pl.CostEstimate(
            flops=8 * rows * depth * width,
            bytes_accessed=2 * (rows * depth + 4 * depth * width + 4 * rows * width),
            transcendentals=0,
        ),
    )(*pieces, *weights)


def attend_kernel(table, x0, x1, x2, x3, query_own, query_oth, kv_own, kv_oth, out, normed):
    width = query_own.shape[1]
    heads = 2 * width // HD
    for k, ref in enumerate((x0, x1, x2, x3)):
        wide = ref[...].astype(F32)
        scale = lax.rsqrt(jnp.mean(wide * wide, -1, keepdims=True) + NORM_EPS)
        normed[k * FR:(k + 1) * FR, :] = (wide * scale).astype(BF16)
    queries = jnp.concatenate(
        [dot(normed[...], query_own[...]), dot(normed[...], query_oth[...])], 1
    ).astype(BF16)
    is_own = table[0] == 1
    column = lax.broadcasted_iota(jnp.int32, (FR, MEMF), 1)
    scores, values = [], []
    for k in range(4):
        place = table[1 + k]
        length = table[5 + k]
        start = pl.multiple_of(place * MEMF, MEMF)
        mine = kv_own[pl.ds(start, MEMF), :]
        other = kv_oth[pl.ds(start, MEMF), :]
        other = jnp.concatenate(
            [other[:, n * width:(n + 1) * width] for n in (1, 0, 3, 2)], 1
        )
        kv = jnp.where(is_own, mine, other)
        values.append(kv[:, 2 * width:])
        for h in range(heads):
            found = lax.dot_general(
                queries[k * FR:(k + 1) * FR, h * HD:(h + 1) * HD],
                kv[:, h * HD:(h + 1) * HD],
                (((1,), (1,)), ((), ())),
                preferred_element_type=F32,
            )
            found = found * (1.0 / math.sqrt(HD))
            scores.append(jnp.where(column < length, found, -jnp.inf))
    score = jnp.concatenate(scores, 0)
    expo = jnp.exp(score - jnp.max(score, -1, keepdims=True))
    probs = (expo / jnp.sum(expo, -1, keepdims=True)).astype(BF16)
    for k in range(4):
        for h in range(heads):
            at = (k * heads + h) * FR
            out[k, :, h * HD:(h + 1) * HD] = dot(
                probs[at:at + FR], values[k][:, h * HD:(h + 1) * HD]
            ).astype(BF16)


def attend(table, pieces, weights, kv_own, kv_oth):
    depth, width = weights[0].shape
    return pl.pallas_call(
        attend_kernel,
        out_shape=jax.ShapeDtypeStruct((4, FR, 2 * width), BF16),
        in_specs=[pl.BlockSpec(memory_space=pltpu.SMEM)] + whole(8),
        out_specs=pl.BlockSpec(memory_space=pltpu.VMEM),
        scratch_shapes=[pltpu.VMEM((4 * FR, depth), BF16)],
        compiler_params=pltpu.CompilerParams(vmem_limit_bytes=VMEM_BYTES),
        cost_estimate=pl.CostEstimate(
            flops=16 * FR * depth * width,
            bytes_accessed=2 * (4 * FR * depth + 2 * depth * width) + 4 * kv_own.size,
            transcendentals=4 * FR * MEMF * 4,
        ),
    )(table, *pieces, *weights, kv_own, kv_oth)


def project_kernel(table, *refs):
    att = refs[:8]
    own, oth, direct, crossed = refs[8], refs[9], refs[10:16], refs[16:22]
    x_ref, out = refs[22:]
    step = pl.program_id(0)
    half_steps = pl.num_programs(0) // 2
    width = own.shape[0]

    def finish(others):
        total = None
        for k in range(4):
            pair = (own, oth) if k == 0 else (others[k - 1], others[k + 2])
            for n, weight in enumerate(pair):
                rows = jnp.concatenate(
                    [att[j * 4 + k][:, n * width:(n + 1) * width] for j in range(2)], 0
                )
                term = dot(rows, weight[...])
                total = term if total is None else total + term
        row = lax.broadcasted_iota(jnp.int32, total.shape, 0)
        limit = jnp.where(row < FR, table[1], table[2] + FR)
        branch = jnp.where(row < limit, total, 0.0)
        out[...] = (x_ref[...].astype(F32) + branch).astype(BF16)

    pl.when(step < half_steps)(lambda: finish(direct))
    pl.when(step >= half_steps)(lambda: finish(crossed))


def project(table, att, own, oth, direct, crossed, x):
    width, depth = own.shape
    rows = x.shape[0]
    tile = 512
    half = depth // 2 // tile

    def placed(i, table):
        group = table[0]
        return 0, jnp.where(i < half, group * half + i, (1 - group) * half + i - half)

    att_specs = [pl.BlockSpec((FR, 2 * width), lambda i, table: (0, 0))] * 8
    full = pl.BlockSpec((width, tile), placed)
    first = pl.BlockSpec((width, tile), lambda i, table: (0, jnp.minimum(i, half - 1)))
    second = pl.BlockSpec((width, tile), lambda i, table: (0, jnp.maximum(i - half, 0)))
    row_block = pl.BlockSpec((rows, tile), placed)
    return pl.pallas_call(
        project_kernel,
        out_shape=jax.ShapeDtypeStruct(x.shape, BF16),
        grid_spec=pltpu.PrefetchScalarGridSpec(
            num_scalar_prefetch=1,
            grid=(2 * half,),
            in_specs=att_specs + [full, full] + [first] * 6 + [second] * 6 + [row_block],
            out_specs=row_block,
        ),
        compiler_params=pltpu.CompilerParams(
            vmem_limit_bytes=VMEM_BYTES, dimension_semantics=("arbitrary",)
        ),
        cost_estimate=pl.CostEstimate(
            flops=16 * rows * width * depth,
            bytes_accessed=2 * (8 * width * depth + 2 * rows * depth),
            transcendentals=0,
        ),
    )(table, *att, own, oth, *direct, *crossed, x)


def shards(arriving, memory, w_query, w_key, w_value, w_out, tok_len, mem_len):
    me = lax.axis_index("section")
    size = lax.axis_size("section")
    section = me // GROUP
    slot = me % GROUP
    core = me & 1
    group = lax.axis_index("groups")
    depth = arriving.shape[1]

    ring = size == MB and memory.shape[0] == MEMF
    if ring:
        pieces = [memory]
        mem_far = flip(memory, FAR)
        mem_near = flip(memory, NEAR)
        mem_hop = hop(memory)
    x_first, x_last = arriving[:FR], arriving[FR:]

    query_pair = [w_query, flip(w_query, CORE)]
    kv_weights = [w_key, flip(w_key, CORE), w_value, flip(w_value, CORE)]
    out_core = flip(w_out, CORE)

    hop_x = [hop(x_first), hop(x_last)]
    if ring:
        mem_first = [memory, mem_near, mem_far, flip(mem_far, NEAR)]
        hop_far = flip(mem_hop, FAR)
        mem_second = [mem_hop, flip(mem_hop, NEAR), hop_far, flip(hop_far, NEAR)]
        place = lambda utt: (utt ^ me) >> 1
    else:
        gathered = lax.all_gather(memory, "section", axis=0, tiled=True)
        gathered = gathered.reshape(MB // 2, 2, MEMF, depth)
        gathered = lax.dynamic_index_in_dim(gathered, core, 1, keepdims=False)
        mem_first = [gathered[k] for k in range(4)]
        mem_second = [gathered[k] for k in range(4, 8)]
        place = lambda utt: utt >> 1
    kv_halves = [keys_values(part, kv_weights) for part in (mem_first, mem_second)]
    kv_own = jnp.concatenate(kv_halves, 0)
    kv_oth = jnp.concatenate([flip(part, CORE) for part in kv_halves], 0)

    half_cols = depth // 2
    half = lax.dynamic_slice_in_dim(w_out, group * half_cols, half_cols, 1)
    out_near = flip(half, NEAR)
    out_far = flip(half, FAR)
    out_diag = flip(out_near, FAR)
    direct = [out_near, out_far, out_diag]
    crossed = [across(part) for part in direct]
    direct = direct + [flip(part, CORE) for part in direct]
    crossed = crossed + [flip(part, CORE) for part in crossed]

    att = []
    for j in range(2):
        own = hop_x[j]
        far = flip(own, FAR)
        rows = [own, flip(own, NEAR), far, flip(far, NEAR)]
        micro = [2 * (slot ^ chip) + j for chip in CHIPS]
        utts = [(section + b) % MB for b in micro]
        is_own = ((section + j) & 1) == core
        table = jnp.stack(
            [is_own.astype(jnp.int32)]
            + [place(utt) for utt in utts]
            + [mem_len[utt] for utt in utts]
        )
        got = attend(table, rows, query_pair, kv_own, kv_oth)
        att += [got[0]] + [flip(got[k], CHIPS[k]) for k in range(1, 4)]

    limits = [tok_len[section * MB + 2 * slot + j] for j in range(2)]
    out_table = jnp.stack([group.astype(jnp.int32)] + limits)
    return project(
        out_table, att, w_out, out_core, direct, crossed, jnp.concatenate(hop_x, 0)
    )


def solution(mesh):
    return jax.shard_map(
        shards,
        mesh=mesh,
        in_specs=(
            P(("groups", "section"), None),
            P(("groups", "section"), None),
            P(None, "section"),
            P(None, "section"),
            P(None, "section"),
            P("section", None),
            P("groups"),
            P("groups"),
        ),
        out_specs=P(("groups", "section"), None),
        check_vma=False,
    )
```

```python
import functools
import math

import jax
import jax.numpy as jnp
from jax import lax
from jax.experimental import pallas as pl
from jax.experimental.pallas import tpu as pltpu
from jax.sharding import PartitionSpec as P

HD = 128
FR = 64
GROUP = 8
MB = 16
MEMF = 64
NORM_EPS = 1e-06
BF16 = jnp.bfloat16
F32 = jnp.float32
VMEM_BYTES = 48 * 2**20

CORE, NEAR, FAR = 1, 2, 4
CHIPS = (0, NEAR, FAR, NEAR | FAR)


def flip(value, bits):
    size = lax.axis_size("section")
    return lax.ppermute(value, "section", [(i, i ^ bits) for i in range(size)])


def hop(value):
    size = lax.axis_size("section")
    return lax.ppermute(value, "section", [(i, (i + GROUP) % size) for i in range(size)])


def after(value, *others):
    return lax.optimization_barrier((value, *others))[0]


def across(value):
    return lax.ppermute(value, "groups", [(0, 1), (1, 0)])


def whole(count):
    return [pl.BlockSpec(memory_space=pltpu.VMEM)] * count


def dot(a, b):
    return jnp.dot(a, b, preferred_element_type=F32)


def keys_values_kernel(*refs):
    *mem_refs, key_own, key_oth, val_own, val_oth, out, rows = refs
    for k, ref in enumerate(mem_refs):
        rows[k * MEMF:(k + 1) * MEMF, :] = ref[:MEMF]
    width = key_own.shape[1]
    for k, weight in enumerate((key_own, key_oth, val_own, val_oth)):
        out[:, k * width:(k + 1) * width] = dot(rows[...], weight[...]).astype(BF16)


def keys_values(pieces, weights):
    depth, width = weights[0].shape
    rows = len(pieces) * MEMF
    return pl.pallas_call(
        keys_values_kernel,
        out_shape=jax.ShapeDtypeStruct((rows, 4 * width), BF16),
        in_specs=whole(len(pieces) + 4),
        out_specs=pl.BlockSpec(memory_space=pltpu.VMEM),
        scratch_shapes=[pltpu.VMEM((rows, depth), BF16)],
        compiler_params=pltpu.CompilerParams(vmem_limit_bytes=VMEM_BYTES),
        cost_estimate=pl.CostEstimate(
            flops=8 * rows * depth * width,
            bytes_accessed=2 * (rows * depth + 4 * depth * width + 4 * rows * width),
            transcendentals=0,
        ),
    )(*pieces, *weights)


def attend_kernel(j, ring, *refs):
    mem_len, x0, x1, x2, x3, query_own, query_oth = refs[:7]
    own_a, own_b, oth_a, oth_b = refs[7:11]
    outs, normed = refs[11:15], refs[15]
    width = query_own.shape[1]
    heads = 2 * width // HD
    me = lax.axis_index("section")
    section, slot, core = me // GROUP, me % GROUP, me % 2
    for k, ref in enumerate((x0, x1, x2, x3)):
        wide = ref[ref.shape[0] - FR:].astype(F32)
        scale = lax.rsqrt(jnp.mean(wide * wide, -1, keepdims=True) + NORM_EPS)
        normed[k * FR:(k + 1) * FR, :] = (wide * scale).astype(BF16)
    queries = jnp.concatenate(
        [dot(normed[...], query_own[...]), dot(normed[...], query_oth[...])], 1
    ).astype(BF16)
    is_own = (section + j) % 2 == core
    column = lax.broadcasted_iota(jnp.int32, (FR, MEMF), 1)
    scores, values = [], []
    for k, chip in enumerate(CHIPS):
        utt = (section + 2 * (slot ^ chip) + j) % MB
        place = (utt ^ me) >> 1 if ring else utt >> 1
        start = pl.multiple_of((place & 3) * MEMF, MEMF)
        here = pl.ds(start, MEMF)
        mine = jnp.where(place < 4, own_a[here, :], own_b[here, :])
        other = jnp.where(place < 4, oth_a[here, :], oth_b[here, :])
        other = jnp.concatenate(
            [other[:, n * width:(n + 1) * width] for n in (1, 0, 3, 2)], 1
        )
        kv = jnp.where(is_own, mine, other)
        length = mem_len[utt]
        values.append(kv[:, 2 * width:])
        for h in range(heads):
            found = lax.dot_general(
                queries[k * FR:(k + 1) * FR, h * HD:(h + 1) * HD],
                kv[:, h * HD:(h + 1) * HD],
                (((1,), (1,)), ((), ())),
                preferred_element_type=F32,
            )
            found = found * (1.0 / math.sqrt(HD))
            scores.append(jnp.where(column < length, found, -jnp.inf))
    score = jnp.concatenate(scores, 0)
    expo = jnp.exp(score - jnp.max(score, -1, keepdims=True))
    probs = (expo / jnp.sum(expo, -1, keepdims=True)).astype(BF16)
    for k in range(4):
        for h in range(heads):
            at = (k * heads + h) * FR
            outs[k][:, h * HD:(h + 1) * HD] = dot(
                probs[at:at + FR], values[k][:, h * HD:(h + 1) * HD]
            ).astype(BF16)


def attend(j, ring, mem_len, pieces, weights, kv):
    depth, width = weights[0].shape
    return pl.pallas_call(
        functools.partial(attend_kernel, j, ring),
        out_shape=[jax.ShapeDtypeStruct((FR, 2 * width), BF16)] * 4,
        in_specs=[pl.BlockSpec(memory_space=pltpu.SMEM)] + whole(10),
        out_specs=whole(4),
        scratch_shapes=[pltpu.VMEM((4 * FR, depth), BF16)],
        compiler_params=pltpu.CompilerParams(vmem_limit_bytes=VMEM_BYTES),
        cost_estimate=pl.CostEstimate(
            flops=16 * FR * depth * width,
            bytes_accessed=2 * (4 * FR * depth + 2 * depth * width) + 8 * kv[0].size,
            transcendentals=4 * FR * MEMF * 4,
        ),
    )(mem_len, *pieces, *weights, *kv)


def project_kernel(group, tok_len, *refs):
    att = refs[:8]
    own, oth, direct, crossed = refs[8], refs[9], refs[10:16], refs[16:22]
    x_first, x_last, out = refs[22:]
    me = lax.axis_index("section")
    step = pl.program_id(0)
    half_steps = pl.num_programs(0) // 2
    width = own.shape[0]
    first_row = (me // GROUP) * MB + 2 * (me % GROUP)

    def finish(others):
        total = None
        for k in range(4):
            pair = (own, oth) if k == 0 else (others[k - 1], others[k + 2])
            for n, weight in enumerate(pair):
                rows = jnp.concatenate(
                    [att[j * 4 + k][:, n * width:(n + 1) * width] for j in range(2)], 0
                )
                term = dot(rows, weight[...])
                total = term if total is None else total + term
        row = lax.broadcasted_iota(jnp.int32, (FR, total.shape[1]), 0)
        for j, x_ref in enumerate((x_first, x_last)):
            branch = jnp.where(row < tok_len[first_row + j], total[j * FR:(j + 1) * FR], 0.0)
            out[j * FR:(j + 1) * FR, :] = (x_ref[...].astype(F32) + branch).astype(BF16)

    pl.when(step < half_steps)(lambda: finish(direct))
    pl.when(step >= half_steps)(lambda: finish(crossed))


def project(group, tok_len, att, own, oth, direct, crossed, x_first, x_last):
    width, depth = own.shape
    rows = 2 * FR
    tile = 512
    half = depth // 2 // tile

    def column(i, group):
        return jnp.where(i < half, group[0] * half + i, (1 - group[0]) * half + i - half)

    att_specs = [pl.BlockSpec((FR, 2 * width), lambda i, group: (0, 0))] * 8
    full = pl.BlockSpec((width, tile), lambda i, group: (0, column(i, group)))
    early = pl.BlockSpec((width, tile), lambda i, group: (0, jnp.minimum(i, half - 1)))
    late = pl.BlockSpec((width, tile), lambda i, group: (0, jnp.maximum(i - half, 0)))
    x_specs = [
        pl.BlockSpec((FR, tile), lambda i, group, at=at: (at, column(i, group)))
        for at in (x_first.shape[0] // FR - 1, x_last.shape[0] // FR - 1)
    ]
    return pl.pallas_call(
        project_kernel,
        out_shape=jax.ShapeDtypeStruct((rows, depth), BF16),
        grid_spec=pltpu.PrefetchScalarGridSpec(
            num_scalar_prefetch=1,
            grid=(2 * half,),
            in_specs=[pl.BlockSpec(memory_space=pltpu.SMEM)]
            + att_specs + [full, full] + [early] * 6 + [late] * 6 + x_specs,
            out_specs=pl.BlockSpec((rows, tile), lambda i, group: (0, column(i, group))),
        ),
        compiler_params=pltpu.CompilerParams(
            vmem_limit_bytes=VMEM_BYTES, dimension_semantics=("arbitrary",)
        ),
        cost_estimate=pl.CostEstimate(
            flops=16 * rows * width * depth,
            bytes_accessed=2 * (8 * width * depth + 2 * rows * depth),
            transcendentals=0,
        ),
    )(group, tok_len, *att, own, oth, *direct, *crossed, x_first, x_last)


def shards(arriving, memory, w_query, w_key, w_value, w_out, tok_len, mem_len):
    me = lax.axis_index("section")
    size = lax.axis_size("section")
    group = lax.axis_index("groups")
    depth = arriving.shape[1]
    half_cols = depth // 2
    ring = size == MB and memory.shape[0] == MEMF
    x_first, x_last = arriving[:FR], arriving[FR:]
    half = lax.dynamic_slice_in_dim(w_out, group * half_cols, half_cols, 1)
    key_oth = flip(w_key, CORE)
    value_oth = flip(after(w_value, key_oth), CORE)
    query_oth = flip(after(w_query, value_oth), CORE)
    out_core = flip(after(w_out, query_oth), CORE)
    kv_weights = [w_key, key_oth, w_value, value_oth]
    query_pair = [w_query, query_oth]

    out_near = flip(half, NEAR)
    if ring:
        mem_far = flip(memory, FAR)
        mem_near = flip(memory, NEAR)
        mem_diag = flip(mem_far, NEAR)
        mem_first = [memory, mem_near, mem_far, mem_diag]
        first_hop = hop(jnp.concatenate([memory, x_first], 0))
    else:
        first_hop = hop(x_first)
        gathered = lax.all_gather(memory, "section", axis=0, tiled=True)
        gathered = gathered.reshape(MB // 2, 2, MEMF, depth)
        gathered = lax.dynamic_index_in_dim(gathered, me & 1, 1, keepdims=False)
        mem_first = [gathered[k] for k in range(4)]
        mem_near, mem_far, mem_diag = mem_first[1:]
    out_far = flip(after(half, mem_near, mem_far), FAR)
    cross_near = across(out_near)

    first_hop_ready = after(first_hop, mem_diag, out_core)
    last_hop = hop(after(x_last, first_hop_ready))
    first_far = flip(first_hop_ready, FAR)
    first_near = flip(first_hop_ready, NEAR)
    kv_first = keys_values(mem_first, kv_weights)
    first_diag = flip(after(first_far, kv_first), NEAR)
    out_diag = flip(after(out_near, first_far), FAR)
    first = [first_hop, first_near, first_far, first_diag]
    cross_far = across(after(out_far, cross_near))
    last_far = flip(after(last_hop, first_near), FAR)
    last_near = flip(after(last_hop, first_near), NEAR)
    last_diag = flip(after(last_far, first_diag), NEAR)
    last = [last_hop, last_near, last_far, last_diag]
    cross_diag = across(after(out_diag, cross_far))

    mem_second = first if ring else [gathered[k] for k in range(4, 8)]
    kv_second = keys_values(mem_second, kv_weights)
    kv = [kv_first, kv_second, flip(kv_first, CORE), flip(kv_second, CORE)]

    direct = [out_near, out_far, out_diag]
    crossed = [cross_near, cross_far, cross_diag]
    direct = direct + [flip(part, CORE) for part in direct]
    crossed = crossed + [flip(part, CORE) for part in crossed]

    att = []
    for j, rows in enumerate((first, last)):
        got = attend(j, ring, mem_len, rows, query_pair, kv)
        att += [got[0]] + [flip(got[k], CHIPS[k]) for k in range(1, 4)]

    limits = tok_len
    return project(
        group.astype(jnp.int32).reshape(1), limits, att, w_out, out_core, direct, crossed, first[0], last[0]
    )


def solution(mesh):
    return jax.shard_map(
        shards,
        mesh=mesh,
        in_specs=(
            P(("groups", "section"), None),
            P(("groups", "section"), None),
            P(None, "section"),
            P(None, "section"),
            P(None, "section"),
            P("section", None),
            P("groups"),
            P("groups"),
        ),
        out_specs=P(("groups", "section"), None),
        check_vma=False,
    )
```

```python
import functools
import math

import jax
import jax.numpy as jnp
from jax import lax
from jax.experimental import pallas as pl
from jax.experimental.pallas import tpu as pltpu
from jax.sharding import PartitionSpec as P

HD = 128
FR = 64
GROUP = 8
MB = 16
MEMF = 64
NORM_EPS = 1e-06
BF16 = jnp.bfloat16
F32 = jnp.float32
VMEM_BYTES = 32 * 2**20
WIDE_VMEM_BYTES = 48 * 2**20

CORE, NEAR, FAR = 1, 2, 4
CHIPS = (0, NEAR, FAR, NEAR | FAR)


def flip(value, bits):
    size = lax.axis_size("section")
    return lax.ppermute(value, "section", [(i, i ^ bits) for i in range(size)])


def hop(value):
    size = lax.axis_size("section")
    return lax.ppermute(value, "section", [(i, (i + GROUP) % size) for i in range(size)])


def after(value, *others):
    return lax.optimization_barrier((value, *others))[0]


def together(*values):
    return lax.optimization_barrier(values)


def across(value):
    return lax.ppermute(value, "groups", [(0, 1), (1, 0)])


def whole(count):
    return [pl.BlockSpec(memory_space=pltpu.VMEM)] * count


def dot(a, b):
    return jnp.dot(a, b, preferred_element_type=F32)


def keys_values_kernel(*refs):
    *mem_refs, key_own, key_oth, val_own, val_oth, out, rows = refs
    for k, ref in enumerate(mem_refs):
        rows[k * MEMF:(k + 1) * MEMF, :] = ref[:MEMF]
    width = key_own.shape[1]
    for k, weight in enumerate((key_own, key_oth, val_own, val_oth)):
        out[:, k * width:(k + 1) * width] = dot(rows[...], weight[...]).astype(BF16)


def keys_values(pieces, weights):
    depth, width = weights[0].shape
    rows = len(pieces) * MEMF
    return pl.pallas_call(
        keys_values_kernel,
        out_shape=jax.ShapeDtypeStruct((rows, 4 * width), BF16),
        in_specs=whole(len(pieces) + 4),
        out_specs=pl.BlockSpec(memory_space=pltpu.VMEM),
        scratch_shapes=[pltpu.VMEM((rows, depth), BF16)],
        compiler_params=pltpu.CompilerParams(vmem_limit_bytes=VMEM_BYTES),
        cost_estimate=pl.CostEstimate(flops=0, bytes_accessed=0, transcendentals=0),
    )(*pieces, *weights)


def attend_kernel(j, ring, *refs):
    mem_len, x0, x1, x2, x3, query_own, query_oth = refs[:7]
    own_a, own_b, oth_a, oth_b = refs[7:11]
    outs, normed = refs[11:13], refs[13]
    width = query_own.shape[1]
    heads = 2 * width // HD
    me = lax.axis_index("section")
    section, slot, core = me // GROUP, me % GROUP, me % 2
    for k, ref in enumerate((x0, x1, x2, x3)):
        wide = ref[ref.shape[0] - FR:].astype(F32)
        scale = lax.rsqrt(jnp.mean(wide * wide, -1, keepdims=True) + NORM_EPS)
        normed[k * FR:(k + 1) * FR, :] = (wide * scale).astype(BF16)
    queries = jnp.concatenate(
        [dot(normed[...], query_own[...]), dot(normed[...], query_oth[...])], 1
    ).astype(BF16)
    is_own = (section + j) % 2 == core
    column = lax.broadcasted_iota(jnp.int32, (FR, MEMF), 1)
    scores, values = [], []
    for k, chip in enumerate(CHIPS):
        utt = (section + 2 * (slot ^ chip) + j) % MB
        place = (utt ^ me) >> 1 if ring else utt >> 1
        start = pl.multiple_of((place & 3) * MEMF, MEMF)
        here = pl.ds(start, MEMF)
        mine = jnp.where(place < 4, own_a[here, :], own_b[here, :])
        other = jnp.where(place < 4, oth_a[here, :], oth_b[here, :])
        other = jnp.concatenate(
            [other[:, n * width:(n + 1) * width] for n in (1, 0, 3, 2)], 1
        )
        kv = jnp.where(is_own, mine, other)
        length = mem_len[utt]
        values.append(kv[:, 2 * width:])
        for h in range(heads):
            found = lax.dot_general(
                queries[k * FR:(k + 1) * FR, h * HD:(h + 1) * HD],
                kv[:, h * HD:(h + 1) * HD],
                (((1,), (1,)), ((), ())),
                preferred_element_type=F32,
            )
            found = found * (1.0 / math.sqrt(HD))
            scores.append(jnp.where(column < length, found, -jnp.inf))
    score = jnp.concatenate(scores, 0)
    expo = jnp.exp(score - jnp.max(score, -1, keepdims=True))
    probs = (expo / jnp.sum(expo, -1, keepdims=True)).astype(BF16)
    for k in range(4):
        for h in range(heads):
            at = (k * heads + h) * FR
            outs[k // 2][k % 2 * FR:(k % 2 + 1) * FR, h * HD:(h + 1) * HD] = dot(
                probs[at:at + FR], values[k][:, h * HD:(h + 1) * HD]
            ).astype(BF16)


def attend(j, ring, mem_len, pieces, weights, kv):
    depth, width = weights[0].shape
    return pl.pallas_call(
        functools.partial(attend_kernel, j, ring),
        out_shape=[jax.ShapeDtypeStruct((2 * FR, 2 * width), BF16)] * 2,
        in_specs=[pl.BlockSpec(memory_space=pltpu.SMEM)] + whole(10),
        out_specs=whole(2),
        scratch_shapes=[pltpu.VMEM((4 * FR, depth), BF16)],
        compiler_params=pltpu.CompilerParams(vmem_limit_bytes=VMEM_BYTES),
        cost_estimate=pl.CostEstimate(flops=0, bytes_accessed=0, transcendentals=0),
    )(mem_len, *pieces, *weights, *kv)


def project_kernel(near, place, tok_len, *refs):
    att = refs[:8]
    own, oth, direct, crossed = refs[8], refs[9], refs[10:16], refs[16:22]
    x_refs, out = refs[22:24], refs[24]
    me = lax.axis_index("section")
    step = pl.program_id(0)
    half_steps = pl.num_programs(0) // 2
    width = own.shape[0]
    slot = (me % GROUP) ^ (NEAR if near else 0)
    first_row = (me // GROUP) * MB + 2 * slot

    def finish(others):
        total = None
        for k in range(4):
            at = FR if near != (k % 2 == 1) else 0
            pair = (own, oth) if k == 0 else (others[k - 1], others[k + 2])
            for n, weight in enumerate(pair):
                rows = jnp.concatenate(
                    [att[j * 4 + k][at:at + FR, n * width:(n + 1) * width] for j in range(2)], 0
                )
                term = dot(rows, weight[...])
                total = term if total is None else total + term
        row = lax.broadcasted_iota(jnp.int32, (FR, total.shape[1]), 0)
        for j, x_ref in enumerate(x_refs):
            branch = jnp.where(row < tok_len[first_row + j], total[j * FR:(j + 1) * FR], 0.0)
            out[j * FR:(j + 1) * FR, :] = (x_ref[...].astype(F32) + branch).astype(BF16)

    pl.when(step < half_steps)(lambda: finish(direct))
    pl.when(step >= half_steps)(lambda: finish(crossed))


def project(near, place, tok_len, att, own, oth, direct, crossed, x_first, x_last):
    width, depth = own.shape
    rows = 2 * FR
    tile = 512
    half = direct[0].shape[1] // tile

    def column(i, place):
        return jnp.where(i < half, place[0] * half + i, (1 - place[0]) * half + i - half)

    def everywhere(i, place):
        return 0, place[1] * 2 * half + column(i, place)

    att_specs = [pl.BlockSpec((2 * FR, 2 * width), lambda i, place: (0, 0))] * 8
    full = pl.BlockSpec((width, tile), everywhere)
    x_specs = [
        pl.BlockSpec((FR, tile), lambda i, place, at=ref.shape[0] // FR - 1: (at, everywhere(i, place)[1]))
        for ref in (x_first, x_last)
    ]
    early = pl.BlockSpec((width, tile), lambda i, place: (0, jnp.minimum(i, half - 1)))
    late = pl.BlockSpec((width, tile), lambda i, place: (0, jnp.maximum(i - half, 0)))
    return pl.pallas_call(
        functools.partial(project_kernel, near),
        out_shape=jax.ShapeDtypeStruct((rows, 2 * half * tile), BF16),
        grid_spec=pltpu.PrefetchScalarGridSpec(
            num_scalar_prefetch=1,
            grid=(2 * half,),
            in_specs=[pl.BlockSpec(memory_space=pltpu.SMEM)]
            + att_specs + [full, full] + [early] * 6 + [late] * 6
            + x_specs,
            out_specs=pl.BlockSpec((rows, tile), lambda i, place: (0, column(i, place))),
        ),
        compiler_params=pltpu.CompilerParams(
            vmem_limit_bytes=WIDE_VMEM_BYTES, dimension_semantics=("arbitrary",)
        ),
        cost_estimate=pl.CostEstimate(flops=0, bytes_accessed=0, transcendentals=0),
    )(place, tok_len, *att, own, oth, *direct, *crossed, x_first, x_last)


def shards(arriving, memory, w_query, w_key, w_value, w_out, tok_len, mem_len):
    me = lax.axis_index("section")
    size = lax.axis_size("section")
    group = lax.axis_index("groups")
    side = (me // NEAR) % 2
    depth = arriving.shape[1]
    ring = size == MB and memory.shape[0] == MEMF

    part_cols = depth // 4
    to_near = lax.dynamic_slice_in_dim(w_out, (2 * (1 - side) + group) * part_cols, part_cols, 1)
    to_far = lax.dynamic_slice_in_dim(w_out, (2 * side + group) * part_cols, part_cols, 1)
    if not ring:
        gathered = lax.all_gather(memory, "section", axis=0, tiled=True)
        gathered = gathered.reshape(MB // 2, 2, MEMF, depth)
        gathered = lax.dynamic_index_in_dim(gathered, me & 1, 1, keepdims=False)
        gathered = [gathered[k] for k in range(MB // 2)]

    out_near = flip(to_near, NEAR)
    key_oth = flip(w_key, CORE)
    if ring:
        mem_hop, mem_near, mem_far = hop(memory), flip(memory, NEAR), flip(memory, FAR)
    else:
        mem_hop = mem_near = mem_far = out_near
    mem_hop, mem_near, mem_far, out_near, key_oth, arriving, w_value = together(
        mem_hop, mem_near, mem_far, out_near, key_oth, arriving, w_value
    )
    first_hop = hop(arriving[:FR])
    value_oth = flip(w_value, CORE)
    if ring:
        hop_far, hop_near, mem_diag = flip(mem_hop, FAR), flip(mem_hop, NEAR), flip(mem_far, NEAR)
    else:
        hop_far = hop_near = mem_diag = mem_far
    first_hop, hop_far, hop_near, mem_diag, value_oth, arriving, out_near = together(
        first_hop, hop_far, hop_near, mem_diag, value_oth, arriving, out_near
    )
    kv_weights = [w_key, key_oth, w_value, value_oth]
    last_hop = hop(arriving[FR:])
    first_far, first_near = flip(first_hop, FAR), flip(first_hop, NEAR)
    hop_diag = flip(hop_far, NEAR) if ring else hop_far
    cross_near = across(out_near)
    mem_first = [memory, mem_near, mem_far, mem_diag] if ring else gathered[:4]
    kv_first = keys_values(mem_first, kv_weights)
    last_hop, first_far, first_near, hop_diag, cross_near, kv_first, to_far, w_query = together(
        last_hop, first_far, first_near, hop_diag, cross_near, kv_first, to_far, w_query
    )
    last_far, last_near, first_diag = flip(last_hop, FAR), flip(last_hop, NEAR), flip(first_far, NEAR)
    out_far = flip(to_far, FAR)
    query_oth = flip(w_query, CORE)
    mem_second = [mem_hop, hop_near, hop_far, hop_diag] if ring else gathered[4:]
    kv_second = keys_values(mem_second, kv_weights)
    last_far, last_near, first_diag, out_far, query_oth, kv_second, kv_first, out_near, w_out = together(
        last_far, last_near, first_diag, out_far, query_oth, kv_second, kv_first, out_near, w_out
    )
    query_pair = [w_query, query_oth]
    last_diag = flip(last_far, NEAR)
    out_diag = flip(out_near, FAR)
    cross_far = across(out_far)
    kv = [kv_first, kv_second, flip(kv_first, CORE), flip(kv_second, CORE)]
    first = [first_hop, first_near, first_far, first_diag]
    here, there = attend(0, ring, mem_len, first, query_pair, kv)
    att = [here, flip(here, NEAR), flip(there, FAR), flip(there, NEAR | FAR)]
    near_core, far_core, cross_core = [
        flip(after(part, kv[2], kv[3]), CORE) for part in (out_near, out_far, cross_near)
    ]
    last_diag, out_diag, cross_far, w_out, near_core, far_core, cross_core, *att[1:] = together(
        last_diag, out_diag, cross_far, w_out, near_core, far_core, cross_core, *att[1:]
    )
    cross_diag = across(out_diag)
    out_core = flip(w_out, CORE)
    last = [last_hop, last_near, last_far, last_diag]
    here, there = attend(1, ring, mem_len, last, query_pair, kv)
    att += [here, flip(here, NEAR), flip(there, FAR), flip(there, NEAR | FAR)]
    rest = [out_diag, cross_far, cross_diag]
    diag_core, cross_far_core, cross_diag_core = [
        flip(part, CORE) for part in together(*rest, *att[5:])[:3]
    ]
    direct = [out_near, out_far, out_diag]
    crossed = [cross_near, cross_far, cross_diag]
    direct_core = [near_core, far_core, diag_core]
    crossed_core = [cross_core, cross_far_core, cross_diag_core]

    place = jnp.stack([group, side]).astype(jnp.int32)
    direct = direct + direct_core
    crossed = crossed + crossed_core
    theirs = project(True, place, tok_len, att, w_out, out_core, direct, crossed, first[1], last[1])
    theirs = flip(theirs, NEAR)
    mine = project(False, place, tok_len, att, w_out, out_core, direct, crossed, first[0], last[0])
    return jnp.where(
        side == 0, jnp.concatenate([mine, theirs], 1), jnp.concatenate([theirs, mine], 1)
    )


def solution(mesh):
    return jax.shard_map(
        shards,
        mesh=mesh,
        in_specs=(
            P(("groups", "section"), None),
            P(("groups", "section"), None),
            P(None, "section"),
            P(None, "section"),
            P(None, "section"),
            P("section", None),
            P("groups"),
            P("groups"),
        ),
        out_specs=P(("groups", "section"), None),
        check_vma=False,
    )
```

```python
import functools
import math

import jax
import jax.numpy as jnp
from jax import lax
from jax.experimental import pallas as pl
from jax.experimental.pallas import tpu as pltpu
from jax.sharding import PartitionSpec as P

HD = 128
FR = 64
GROUP = 8
MB = 16
MEMF = 64
NORM_EPS = 1e-06
BF16 = jnp.bfloat16
F32 = jnp.float32
VMEM_BYTES = 32 * 2**20
WIDE_VMEM_BYTES = 58 * 2**20

CORE, NEAR, FAR = 1, 2, 4
CHIPS = (0, NEAR, FAR, NEAR | FAR)


def flip(value, bits):
    size = lax.axis_size("section")
    return lax.ppermute(value, "section", [(i, i ^ bits) for i in range(size)])


def hop(value):
    size = lax.axis_size("section")
    return lax.ppermute(value, "section", [(i, (i + GROUP) % size) for i in range(size)])


def after(value, *others):
    return lax.optimization_barrier((value, *others))[0]


def together(*values):
    return lax.optimization_barrier(values)


def across(value):
    return lax.ppermute(value, "groups", [(0, 1), (1, 0)])


def whole(count):
    return [pl.BlockSpec(memory_space=pltpu.VMEM)] * count


def dot(a, b):
    return jnp.dot(a, b, preferred_element_type=F32)


def keys_values_kernel(*refs):
    *mem_refs, key_own, val_own, pair_oth = refs[:7]
    earlier, out, rows = refs[7:-2], refs[-2], refs[-1]
    done = earlier[0].shape[0] if earlier else 0
    if earlier:
        out[:done, :] = earlier[0][...]
    for k, ref in enumerate(mem_refs):
        rows[k * MEMF:(k + 1) * MEMF, :] = ref[:MEMF]
    width = key_own.shape[1]
    weights = (key_own[...], pair_oth[:, :width], val_own[...], pair_oth[:, width:])
    for k, weight in enumerate(weights):
        out[done:, k * width:(k + 1) * width] = dot(rows[...], weight).astype(BF16)


def keys_values(pieces, weights, *earlier):
    depth, width = weights[0].shape
    rows = len(pieces) * MEMF
    total = rows + sum(part.shape[0] for part in earlier)
    return pl.pallas_call(
        keys_values_kernel,
        out_shape=jax.ShapeDtypeStruct((total, 4 * width), BF16),
        in_specs=whole(len(pieces) + 3 + len(earlier)),
        out_specs=pl.BlockSpec(memory_space=pltpu.VMEM),
        scratch_shapes=[pltpu.VMEM((rows, depth), BF16)],
        compiler_params=pltpu.CompilerParams(vmem_limit_bytes=VMEM_BYTES),
        cost_estimate=pl.CostEstimate(flops=0, bytes_accessed=0, transcendentals=0),
    )(*pieces, *weights, *earlier)


def attend_kernel(j, ring, *refs):
    mem_len, x0, x1, x2, x3, query_own, query_oth = refs[:7]
    kv_own, kv_oth = refs[7:9]
    outs, normed = refs[9:11], refs[11]
    width = query_own.shape[1]
    heads = 2 * width // HD
    me = lax.axis_index("section")
    section, slot, core = me // GROUP, me % GROUP, me % 2
    for k, ref in enumerate((x0, x1, x2, x3)):
        wide = ref[ref.shape[0] - FR:].astype(F32)
        scale = lax.rsqrt(jnp.mean(wide * wide, -1, keepdims=True) + NORM_EPS)
        normed[k * FR:(k + 1) * FR, :] = (wide * scale).astype(BF16)
    queries = jnp.concatenate(
        [dot(normed[...], query_own[...]), dot(normed[...], query_oth[...])], 1
    ).astype(BF16)
    is_own = (section + j) % 2 == core
    column = lax.broadcasted_iota(jnp.int32, (FR, MEMF), 1)
    scores, values = [], []
    for k, chip in enumerate(CHIPS):
        utt = (section + 2 * (slot ^ chip) + j) % MB
        place = (utt ^ me) >> 1 if ring else utt >> 1
        here = pl.ds(pl.multiple_of(place * MEMF, MEMF), MEMF)
        mine, other = kv_own[here, :], kv_oth[here, :]
        other = jnp.concatenate(
            [other[:, n * width:(n + 1) * width] for n in (1, 0, 3, 2)], 1
        )
        kv = jnp.where(is_own, mine, other)
        length = mem_len[utt]
        values.append(kv[:, 2 * width:])
        for h in range(heads):
            found = lax.dot_general(
                queries[k * FR:(k + 1) * FR, h * HD:(h + 1) * HD],
                kv[:, h * HD:(h + 1) * HD],
                (((1,), (1,)), ((), ())),
                preferred_element_type=F32,
            )
            found = found * (1.0 / math.sqrt(HD))
            scores.append(jnp.where(column < length, found, -jnp.inf))
    score = jnp.concatenate(scores, 0)
    expo = jnp.exp(score - jnp.max(score, -1, keepdims=True))
    probs = (expo / jnp.sum(expo, -1, keepdims=True)).astype(BF16)
    for k in range(4):
        for h in range(heads):
            at = (k * heads + h) * FR
            outs[k // 2][k % 2 * FR:(k % 2 + 1) * FR, h * HD:(h + 1) * HD] = dot(
                probs[at:at + FR], values[k][:, h * HD:(h + 1) * HD]
            ).astype(BF16)


def attend(j, ring, mem_len, pieces, weights, kv):
    depth, width = weights[0].shape
    return pl.pallas_call(
        functools.partial(attend_kernel, j, ring),
        out_shape=[jax.ShapeDtypeStruct((2 * FR, 2 * width), BF16)] * 2,
        in_specs=[pl.BlockSpec(memory_space=pltpu.SMEM)] + whole(8),
        out_specs=whole(2),
        scratch_shapes=[pltpu.VMEM((4 * FR, depth), BF16)],
        compiler_params=pltpu.CompilerParams(vmem_limit_bytes=VMEM_BYTES),
        cost_estimate=pl.CostEstimate(flops=0, bytes_accessed=0, transcendentals=0),
    )(mem_len, *pieces, *weights, *kv)


def project_kernel(near, place, tok_len, *refs):
    att, weights, x_refs, out = refs[:8], refs[8:16], refs[16:18], refs[18]
    me = lax.axis_index("section")
    width = weights[0].shape[0]
    slot = (me % GROUP) ^ (NEAR if near else 0)
    first_row = (me // GROUP) * MB + 2 * slot
    total = None
    for k in range(4):
        at = FR if near != (k % 2 == 1) else 0
        for n in range(2):
            rows = jnp.concatenate(
                [att[j * 4 + k][at:at + FR, n * width:(n + 1) * width] for j in range(2)], 0
            )
            term = dot(rows, weights[4 * n + k][...])
            total = term if total is None else total + term
    row = lax.broadcasted_iota(jnp.int32, (FR, total.shape[1]), 0)
    for j, x_ref in enumerate(x_refs):
        branch = jnp.where(row < tok_len[first_row + j], total[j * FR:(j + 1) * FR], 0.0)
        out[j * FR:(j + 1) * FR, :] = (x_ref[...].astype(F32) + branch).astype(BF16)


def project(near, place, tok_len, att, own, oth, pieces, x_first, x_last):
    width, depth = own.shape
    rows = 2 * FR
    tile = 512
    steps = pieces[0][0].shape[1] // tile

    def everywhere(i, place):
        return 0, place[0] * steps + i

    def here(i, place):
        return 0, i

    att_specs = [pl.BlockSpec((2 * FR, 2 * width), lambda i, place: (0, 0))] * 8
    full = pl.BlockSpec((width, tile), everywhere)
    parts = [
        pl.BlockSpec((width, tile), lambda i, place, block=block: (block, i)) for _, block in pieces
    ]
    x_specs = [
        pl.BlockSpec((FR, tile), lambda i, place, at=ref.shape[0] // FR - 1: (at, everywhere(i, place)[1]))
        for ref in (x_first, x_last)
    ]
    arrays = [array for array, _ in pieces]
    weights = [own, *arrays[:3], oth, *arrays[3:]]
    return pl.pallas_call(
        functools.partial(project_kernel, near),
        out_shape=jax.ShapeDtypeStruct((rows, steps * tile), BF16),
        grid_spec=pltpu.PrefetchScalarGridSpec(
            num_scalar_prefetch=1,
            grid=(steps,),
            in_specs=[pl.BlockSpec(memory_space=pltpu.SMEM)]
            + att_specs + [full, *parts[:3], full, *parts[3:]] + x_specs,
            out_specs=pl.BlockSpec((rows, tile), here),
        ),
        compiler_params=pltpu.CompilerParams(
            vmem_limit_bytes=WIDE_VMEM_BYTES, dimension_semantics=("arbitrary",)
        ),
        cost_estimate=pl.CostEstimate(flops=0, bytes_accessed=0, transcendentals=0),
    )(place, tok_len, *att, *weights, x_first, x_last)


def assemble_kernel(order, *refs):
    out = refs[-1]
    cols = refs[0].shape[1]
    for k, ref in enumerate(refs[:-1]):
        out[:, pl.ds(pl.multiple_of(order[k] * cols, 128), cols)] = ref[...]


def assemble(order, parts):
    rows, cols = parts[0].shape
    return pl.pallas_call(
        assemble_kernel,
        out_shape=jax.ShapeDtypeStruct((rows, len(parts) * cols), BF16),
        in_specs=[pl.BlockSpec(memory_space=pltpu.SMEM)] + whole(len(parts)),
        out_specs=pl.BlockSpec(memory_space=pltpu.VMEM),
        compiler_params=pltpu.CompilerParams(vmem_limit_bytes=VMEM_BYTES),
    )(order, *parts)


def shards(arriving, memory, w_query, w_key, w_value, w_out, tok_len, mem_len):
    me = lax.axis_index("section")
    size = lax.axis_size("section")
    group = lax.axis_index("groups")
    side = (me // NEAR) % 2
    depth = arriving.shape[1]
    ring = size == MB and memory.shape[0] == MEMF

    part_cols = depth // 4
    to_near = lax.dynamic_slice_in_dim(w_out, (2 * (1 - side) + group) * part_cols, part_cols, 1)
    to_far = lax.dynamic_slice_in_dim(w_out, (2 * side + group) * part_cols, part_cols, 1)
    if not ring:
        gathered = lax.all_gather(memory, "section", axis=0, tiled=True)
        gathered = gathered.reshape(MB // 2, 2, MEMF, depth)
        gathered = lax.dynamic_index_in_dim(gathered, me & 1, 1, keepdims=False)
        gathered = [gathered[k] for k in range(MB // 2)]

    out_near = flip(to_near, NEAR)
    out_core = flip(w_out, CORE)
    kv_pair = jnp.concatenate([w_key, w_value], 1)
    if ring:
        mem_hop, mem_near, mem_far = hop(memory), flip(memory, NEAR), flip(memory, FAR)
    else:
        mem_hop = mem_near = mem_far = out_near
    mem_hop, mem_near, mem_far, out_near, out_core, arriving, kv_pair = together(
        mem_hop, mem_near, mem_far, out_near, out_core, arriving, kv_pair
    )
    first_hop = hop(arriving[:FR])
    kv_pair = flip(kv_pair, CORE)
    if ring:
        hop_far, hop_near, mem_diag = flip(mem_hop, FAR), flip(mem_hop, NEAR), flip(mem_far, NEAR)
    else:
        hop_far = hop_near = mem_diag = mem_far
    first_hop, hop_far, hop_near, mem_diag, kv_pair, arriving, out_near = together(
        first_hop, hop_far, hop_near, mem_diag, kv_pair, arriving, out_near
    )
    kv_weights = [w_key, w_value, kv_pair]
    last_hop = hop(arriving[FR:])
    first_far, first_near = flip(first_hop, FAR), flip(first_hop, NEAR)
    hop_diag = flip(hop_far, NEAR) if ring else hop_far
    cross_near = across(out_near)
    mem_first = [memory, mem_near, mem_far, mem_diag] if ring else gathered[:4]
    kv_first = keys_values(mem_first, kv_weights)
    last_hop, first_far, first_near, hop_diag, cross_near, kv_first, to_far, w_query = together(
        last_hop, first_far, first_near, hop_diag, cross_near, kv_first, to_far, w_query
    )
    last_far, last_near, first_diag = flip(last_hop, FAR), flip(last_hop, NEAR), flip(first_far, NEAR)
    out_far = flip(to_far, FAR)
    query_oth = flip(w_query, CORE)
    mem_second = [mem_hop, hop_near, hop_far, hop_diag] if ring else gathered[4:]
    kv_second = keys_values(mem_second, kv_weights, kv_first)
    last_far, last_near, first_diag, out_far, query_oth, kv_second, out_near = together(
        last_far, last_near, first_diag, out_far, query_oth, kv_second, out_near
    )
    query_pair = [w_query, query_oth]
    last_diag = flip(last_far, NEAR)
    out_diag = flip(out_near, FAR)
    cross_far = across(out_far)
    kv = [kv_second, flip(kv_second, CORE)]
    first = [first_hop, first_near, first_far, first_diag]
    here, there = attend(0, ring, mem_len, first, query_pair, kv)
    att = [here, flip(here, NEAR), flip(there, FAR), flip(there, NEAR | FAR)]
    last_diag, out_diag, cross_far, *att[1:] = together(
        last_diag, out_diag, cross_far, *att[1:]
    )
    cross_diag = across(out_diag)
    direct_core = flip(jnp.concatenate([out_near, out_far, out_diag], 0), CORE)
    last = [last_hop, last_near, last_far, last_diag]
    here, there = attend(1, ring, mem_len, last, query_pair, kv)
    att += [here, flip(here, NEAR), flip(there, FAR), flip(there, NEAR | FAR)]
    crossed_core = flip(after(jnp.concatenate([cross_near, cross_far], 0), *att[5:]), CORE)
    fetched = [(out_near, 0), (out_far, 0), (out_diag, 0)] + [(direct_core, k) for k in range(3)]
    handed = [(cross_near, 0), (cross_far, 0), (cross_diag, 0)]
    handed += [(crossed_core, 0), (crossed_core, 1), (flip(after(cross_diag, *att[5:]), CORE), 0)]

    quarters = jnp.stack(
        [2 * side + group, 2 * side + 1 - group, 2 - 2 * side + group, 3 - 2 * side - group]
    ).astype(jnp.int32)
    def part(near, n, pieces, *others):
        at = 1 if near else 0
        return project(
            near, after(quarters[n:n + 1], *others), tok_len, att, w_out, out_core, pieces, first[at], last[at]
        )

    theirs_b = flip(part(True, 1, handed), NEAR)
    theirs_a = flip(part(True, 0, fetched), NEAR)
    mine = [part(False, 0, fetched), part(False, 1, handed)]
    return assemble(quarters, mine + [theirs_a, theirs_b])


def solution(mesh):
    return jax.shard_map(
        shards,
        mesh=mesh,
        in_specs=(
            P(("groups", "section"), None),
            P(("groups", "section"), None),
            P(None, "section"),
            P(None, "section"),
            P(None, "section"),
            P("section", None),
            P("groups"),
            P("groups"),
        ),
        out_specs=P(("groups", "section"), None),
        check_vma=False,
    )
```

```python
import functools
import math

import jax
import jax.numpy as jnp
from jax import lax
from jax.experimental import pallas as pl
from jax.experimental.pallas import tpu as pltpu
from jax.sharding import PartitionSpec as P

HD = 128
FR = 64
GROUP = 8
MB = 16
MEMF = 64
NORM_EPS = 1e-06
BF16 = jnp.bfloat16
F32 = jnp.float32
VMEM_BYTES = 32 * 2**20
WIDE_VMEM_BYTES = 52 * 2**20

CORE, NEAR, FAR = 1, 2, 4
CHIPS = (0, NEAR, FAR, NEAR | FAR)


def flip(value, bits):
    size = lax.axis_size("section")
    return lax.ppermute(value, "section", [(i, i ^ bits) for i in range(size)])


def hop(value):
    size = lax.axis_size("section")
    return lax.ppermute(value, "section", [(i, (i + GROUP) % size) for i in range(size)])


def after(value, *others):
    return lax.optimization_barrier((value, *others))[0]


def together(*values):
    return lax.optimization_barrier(values)


def across(value):
    return lax.ppermute(value, "groups", [(0, 1), (1, 0)])


def whole(count):
    return [pl.BlockSpec(memory_space=pltpu.VMEM)] * count


def dot(a, b):
    return jnp.dot(a, b, preferred_element_type=F32)


def keys_values_kernel(*refs):
    *mem_refs, key_own, val_own, pair_oth = refs[:7]
    earlier, out, rows = refs[7:-2], refs[-2], refs[-1]
    done = earlier[0].shape[0] if earlier else 0
    if earlier:
        out[:done, :] = earlier[0][...]
    for k, ref in enumerate(mem_refs):
        rows[k * MEMF:(k + 1) * MEMF, :] = ref[:MEMF]
    width = key_own.shape[1]
    weights = (key_own[...], pair_oth[:, :width], val_own[...], pair_oth[:, width:])
    for k, weight in enumerate(weights):
        out[done:, k * width:(k + 1) * width] = dot(rows[...], weight).astype(BF16)


def keys_values(pieces, weights, *earlier):
    depth, width = weights[0].shape
    rows = len(pieces) * MEMF
    total = rows + sum(part.shape[0] for part in earlier)
    return pl.pallas_call(
        keys_values_kernel,
        out_shape=jax.ShapeDtypeStruct((total, 4 * width), BF16),
        in_specs=whole(len(pieces) + 3 + len(earlier)),
        out_specs=pl.BlockSpec(memory_space=pltpu.VMEM),
        scratch_shapes=[pltpu.VMEM((rows, depth), BF16)],
        compiler_params=pltpu.CompilerParams(vmem_limit_bytes=VMEM_BYTES),
        cost_estimate=pl.CostEstimate(flops=0, bytes_accessed=0, transcendentals=0),
    )(*pieces, *weights, *earlier)


def attend_kernel(j, ring, *refs):
    mem_len, x0, x1, x2, x3, query_own, query_oth = refs[:7]
    kv_own, kv_oth = refs[7:9]
    outs, normed = refs[9:11], refs[11]
    width = query_own.shape[1]
    heads = 2 * width // HD
    me = lax.axis_index("section")
    section, slot, core = me // GROUP, me % GROUP, me % 2
    for k, ref in enumerate((x0, x1, x2, x3)):
        wide = ref[ref.shape[0] - FR:].astype(F32)
        scale = lax.rsqrt(jnp.mean(wide * wide, -1, keepdims=True) + NORM_EPS)
        normed[k * FR:(k + 1) * FR, :] = (wide * scale).astype(BF16)
    queries = jnp.concatenate(
        [dot(normed[...], query_own[...]), dot(normed[...], query_oth[...])], 1
    ).astype(BF16)
    is_own = (section + j) % 2 == core
    column = lax.broadcasted_iota(jnp.int32, (FR, MEMF), 1)
    scores, values = [], []
    for k, chip in enumerate(CHIPS):
        utt = (section + 2 * (slot ^ chip) + j) % MB
        place = (utt ^ me) >> 1 if ring else utt >> 1
        here = pl.ds(pl.multiple_of(place * MEMF, MEMF), MEMF)
        mine, other = kv_own[here, :], kv_oth[here, :]
        other = jnp.concatenate(
            [other[:, n * width:(n + 1) * width] for n in (1, 0, 3, 2)], 1
        )
        kv = jnp.where(is_own, mine, other)
        length = mem_len[utt]
        values.append(kv[:, 2 * width:])
        for h in range(heads):
            found = lax.dot_general(
                queries[k * FR:(k + 1) * FR, h * HD:(h + 1) * HD],
                kv[:, h * HD:(h + 1) * HD],
                (((1,), (1,)), ((), ())),
                preferred_element_type=F32,
            )
            found = found * (1.0 / math.sqrt(HD))
            scores.append(jnp.where(column < length, found, -jnp.inf))
    score = jnp.concatenate(scores, 0)
    expo = jnp.exp(score - jnp.max(score, -1, keepdims=True))
    probs = (expo / jnp.sum(expo, -1, keepdims=True)).astype(BF16)
    for k in range(4):
        for h in range(heads):
            at = (k * heads + h) * FR
            outs[k // 2][k % 2 * FR:(k % 2 + 1) * FR, h * HD:(h + 1) * HD] = dot(
                probs[at:at + FR], values[k][:, h * HD:(h + 1) * HD]
            ).astype(BF16)


def attend(j, ring, mem_len, pieces, weights, kv):
    depth, width = weights[0].shape
    return pl.pallas_call(
        functools.partial(attend_kernel, j, ring),
        out_shape=[jax.ShapeDtypeStruct((2 * FR, 2 * width), BF16)] * 2,
        in_specs=[pl.BlockSpec(memory_space=pltpu.SMEM)] + whole(8),
        out_specs=whole(2),
        scratch_shapes=[pltpu.VMEM((4 * FR, depth), BF16)],
        compiler_params=pltpu.CompilerParams(vmem_limit_bytes=VMEM_BYTES),
        cost_estimate=pl.CostEstimate(flops=0, bytes_accessed=0, transcendentals=0),
    )(mem_len, *pieces, *weights, *kv)


def project_kernel(near, place, tok_len, *refs):
    att, weights, x_refs, out = refs[:8], refs[8:-3], refs[-3:-1], refs[-1]
    me = lax.axis_index("section")
    slot = (me % GROUP) ^ (NEAR if near else 0)
    first_row = (me // GROUP) * MB + 2 * slot
    width = att[0].shape[1] // 2
    columns = []
    for n in range(2):
        for k in range(4):
            at = FR if near != (k % 2 == 1) else 0
            columns.append(jnp.concatenate(
                [att[j * 4 + k][at:at + FR, n * width:(n + 1) * width] for j in range(2)], 0
            ))
    total, done = None, 0
    for weight in weights:
        count = weight.shape[0] // width
        term = dot(jnp.concatenate(columns[done:done + count], 1), weight[...])
        total = term if total is None else total + term
        done += count
    row = lax.broadcasted_iota(jnp.int32, (FR, total.shape[1]), 0)
    for j, x_ref in enumerate(x_refs):
        branch = jnp.where(row < tok_len[first_row + j], total[j * FR:(j + 1) * FR], 0.0)
        out[j * FR:(j + 1) * FR, :] = (x_ref[...].astype(F32) + branch).astype(BF16)


def project(near, place, tok_len, att, own, oth, pieces, x_first, x_last):
    width, depth = own.shape
    rows = 2 * FR
    tile = 512
    cols = pieces[0][0].shape[1]
    steps = cols // tile

    def everywhere(i, place):
        return 0, place[0] * steps + i

    def here(i, place):
        return 0, i

    att_specs = [pl.BlockSpec((2 * FR, 2 * width), lambda i, place: (0, 0))] * 8
    weights, weight_specs = [], []
    for mine, others in zip((own, oth), pieces):
        weights += [mine, *others]
        weight_specs.append(pl.BlockSpec((width, tile), everywhere))
        weight_specs += [pl.BlockSpec((other.shape[0], tile), here) for other in others]
    x_specs = [
        pl.BlockSpec((FR, tile), lambda i, place, at=ref.shape[0] // FR - 1: (at, everywhere(i, place)[1]))
        for ref in (x_first, x_last)
    ]
    return pl.pallas_call(
        functools.partial(project_kernel, near),
        out_shape=jax.ShapeDtypeStruct((rows, cols), BF16),
        grid_spec=pltpu.PrefetchScalarGridSpec(
            num_scalar_prefetch=1,
            grid=(steps,),
            in_specs=[pl.BlockSpec(memory_space=pltpu.SMEM)] + att_specs + weight_specs + x_specs,
            out_specs=pl.BlockSpec((rows, tile), here),
        ),
        compiler_params=pltpu.CompilerParams(
            vmem_limit_bytes=WIDE_VMEM_BYTES, dimension_semantics=("arbitrary",)
        ),
        cost_estimate=pl.CostEstimate(flops=0, bytes_accessed=0, transcendentals=0),
    )(place, tok_len, *att, *weights, x_first, x_last)


def assemble_kernel(order, *refs):
    out = refs[-1]
    cols = refs[0].shape[1]
    for k, ref in enumerate(refs[:-1]):
        out[:, pl.ds(pl.multiple_of(order[k] * cols, 128), cols)] = ref[...]


def assemble(order, parts):
    rows, cols = parts[0].shape
    return pl.pallas_call(
        assemble_kernel,
        out_shape=jax.ShapeDtypeStruct((rows, len(parts) * cols), BF16),
        in_specs=[pl.BlockSpec(memory_space=pltpu.SMEM)] + whole(len(parts)),
        out_specs=pl.BlockSpec(memory_space=pltpu.VMEM),
        compiler_params=pltpu.CompilerParams(vmem_limit_bytes=VMEM_BYTES),
    )(order, *parts)


def shards(arriving, memory, w_query, w_key, w_value, w_out, tok_len, mem_len):
    me = lax.axis_index("section")
    size = lax.axis_size("section")
    group = lax.axis_index("groups")
    side = (me // NEAR) % 2
    depth = arriving.shape[1]
    ring = size == MB and memory.shape[0] == MEMF

    part_cols = depth // 4
    to_near = lax.dynamic_slice_in_dim(w_out, (2 * (1 - side) + group) * part_cols, part_cols, 1)
    to_far = lax.dynamic_slice_in_dim(w_out, (2 * side + group) * part_cols, part_cols, 1)
    if not ring:
        gathered = lax.all_gather(memory, "section", axis=0, tiled=True)
        gathered = gathered.reshape(MB // 2, 2, MEMF, depth)
        gathered = lax.dynamic_index_in_dim(gathered, me & 1, 1, keepdims=False)
        gathered = [gathered[k] for k in range(MB // 2)]

    out_near = flip(to_near, NEAR)
    out_core = flip(w_out, CORE)
    kv_pair = jnp.concatenate([w_key, w_value], 1)
    if ring:
        mem_hop, mem_near, mem_far = hop(memory), flip(memory, NEAR), flip(memory, FAR)
    else:
        mem_hop = mem_near = mem_far = out_near
    mem_hop, mem_near, mem_far, out_near, out_core, arriving, kv_pair = together(
        mem_hop, mem_near, mem_far, out_near, out_core, arriving, kv_pair
    )
    first_hop = hop(arriving[:FR])
    kv_pair = flip(kv_pair, CORE)
    if ring:
        hop_far, hop_near, mem_diag = flip(mem_hop, FAR), flip(mem_hop, NEAR), flip(mem_far, NEAR)
    else:
        hop_far = hop_near = mem_diag = mem_far
    first_hop, hop_far, hop_near, mem_diag, kv_pair, arriving, out_near = together(
        first_hop, hop_far, hop_near, mem_diag, kv_pair, arriving, out_near
    )
    kv_weights = [w_key, w_value, kv_pair]
    last_hop = hop(arriving[FR:])
    first_far, first_near = flip(first_hop, FAR), flip(first_hop, NEAR)
    hop_diag = flip(hop_far, NEAR) if ring else hop_far
    cross_near = across(out_near)
    mem_first = [memory, mem_near, mem_far, mem_diag] if ring else gathered[:4]
    kv_first = keys_values(mem_first, kv_weights)
    last_hop, first_far, first_near, hop_diag, cross_near, kv_first, to_far, w_query = together(
        last_hop, first_far, first_near, hop_diag, cross_near, kv_first, to_far, w_query
    )
    last_far, last_near, first_diag = flip(last_hop, FAR), flip(last_hop, NEAR), flip(first_far, NEAR)
    out_far = flip(to_far, FAR)
    query_oth = flip(w_query, CORE)
    mem_second = [mem_hop, hop_near, hop_far, hop_diag] if ring else gathered[4:]
    kv_second = keys_values(mem_second, kv_weights, kv_first)
    last_far, last_near, first_diag, out_far, query_oth, kv_second, out_near = together(
        last_far, last_near, first_diag, out_far, query_oth, kv_second, out_near
    )
    query_pair = [w_query, query_oth]
    last_diag = flip(last_far, NEAR)
    out_diag = flip(out_near, FAR)
    cross_far = across(out_far)
    kv = [kv_second, flip(kv_second, CORE)]
    first = [first_hop, first_near, first_far, first_diag]
    here, there = attend(0, ring, mem_len, first, query_pair, kv)
    att = [here, flip(here, NEAR), flip(there, FAR), flip(there, NEAR | FAR)]
    last_diag, out_diag, cross_far, *att[1:3] = together(
        last_diag, out_diag, cross_far, *att[1:3]
    )
    cross_diag = across(out_diag)
    last = [last_hop, last_near, last_far, last_diag]
    here, there = attend(1, ring, mem_len, last, query_pair, kv)
    att += [here, flip(here, NEAR), flip(there, FAR), flip(there, NEAR | FAR)]
    fetched = jnp.concatenate([out_near, out_far, out_diag], 0)
    crossed = jnp.concatenate([cross_near, cross_far], 0)
    fetched, crossed, cross_diag = together(fetched, crossed, cross_diag, att[3], *att[5:])[:3]
    fetched = [[fetched], [flip(fetched, CORE)]]
    handed = [[crossed, cross_diag], [flip(crossed, CORE), flip(cross_diag, CORE)]]
    quarters = jnp.stack(
        [2 * side + group, 2 * side + 1 - group, 2 - 2 * side + group, 3 - 2 * side - group]
    ).astype(jnp.int32)
    def part(near, n, pieces, *others):
        at = 1 if near else 0
        return project(
            near, after(quarters[n:n + 1], *others), tok_len, att, w_out, out_core, pieces, first[at], last[at]
        )

    theirs_b = flip(part(True, 1, handed), NEAR)
    theirs_a = flip(part(True, 0, fetched), NEAR)
    mine = [part(False, 0, fetched), part(False, 1, handed)]
    return assemble(quarters, mine + [theirs_a, theirs_b])


def solution(mesh):
    return jax.shard_map(
        shards,
        mesh=mesh,
        in_specs=(
            P(("groups", "section"), None),
            P(("groups", "section"), None),
            P(None, "section"),
            P(None, "section"),
            P(None, "section"),
            P("section", None),
            P("groups"),
            P("groups"),
        ),
        out_specs=P(("groups", "section"), None),
        check_vma=False,
    )
```

```python
import functools
import math

import jax
import jax.numpy as jnp
from jax import lax
from jax.experimental import pallas as pl
from jax.experimental.pallas import tpu as pltpu
from jax.sharding import PartitionSpec as P

HD = 128
FR = 64
GROUP = 8
MB = 16
MEMF = 64
NORM_EPS = 1e-06
BF16 = jnp.bfloat16
F32 = jnp.float32
VMEM_BYTES = 32 * 2**20
WIDE_VMEM_BYTES = 52 * 2**20

CORE, NEAR, FAR = 1, 2, 4
CHIPS = (0, NEAR, FAR, NEAR | FAR)


def flip(value, bits):
    size = lax.axis_size("section")
    return lax.ppermute(value, "section", [(i, i ^ bits) for i in range(size)])


def hop(value):
    size = lax.axis_size("section")
    return lax.ppermute(value, "section", [(i, (i + GROUP) % size) for i in range(size)])


def after(value, *others):
    return lax.optimization_barrier((value, *others))[0]


def together(*values):
    return lax.optimization_barrier(values)


def across(value):
    return lax.ppermute(value, "groups", [(0, 1), (1, 0)])


def whole(count):
    return [pl.BlockSpec(memory_space=pltpu.VMEM)] * count


def dot(a, b):
    return jnp.dot(a, b, preferred_element_type=F32)


def keys_values_kernel(*refs):
    *mem_refs, key_own, val_own, pair_oth = refs[:7]
    earlier, out, rows = refs[7:-2], refs[-2], refs[-1]
    done = earlier[0].shape[0] if earlier else 0
    if earlier:
        out[:done, :] = earlier[0][...]
    for k, ref in enumerate(mem_refs):
        rows[k * MEMF:(k + 1) * MEMF, :] = ref[:MEMF]
    width = key_own.shape[1]
    weights = (key_own[...], pair_oth[:, :width], val_own[...], pair_oth[:, width:2 * width])
    for k, weight in enumerate(weights):
        out[done:, k * width:(k + 1) * width] = dot(rows[...], weight).astype(BF16)


def keys_values(pieces, weights, *earlier):
    depth, width = weights[0].shape
    rows = len(pieces) * MEMF
    total = rows + sum(part.shape[0] for part in earlier)
    return pl.pallas_call(
        keys_values_kernel,
        out_shape=jax.ShapeDtypeStruct((total, 4 * width), BF16),
        in_specs=whole(len(pieces) + 3 + len(earlier)),
        out_specs=pl.BlockSpec(memory_space=pltpu.VMEM),
        scratch_shapes=[pltpu.VMEM((rows, depth), BF16)],
        compiler_params=pltpu.CompilerParams(vmem_limit_bytes=VMEM_BYTES),
        cost_estimate=pl.CostEstimate(flops=0, bytes_accessed=0, transcendentals=0),
    )(*pieces, *weights, *earlier)


def attend_kernel(j, ring, *refs):
    mem_len, x0, x1, x2, x3, query_own, query_oth = refs[:7]
    kv_own, kv_oth = refs[7:9]
    outs, normed = refs[9:11], refs[11]
    width = query_own.shape[1]
    heads = 2 * width // HD
    me = lax.axis_index("section")
    section, slot, core = me // GROUP, me % GROUP, me % 2
    for k, ref in enumerate((x0, x1, x2, x3)):
        wide = ref[ref.shape[0] - FR:].astype(F32)
        scale = lax.rsqrt(jnp.mean(wide * wide, -1, keepdims=True) + NORM_EPS)
        normed[k * FR:(k + 1) * FR, :] = (wide * scale).astype(BF16)
    queries = jnp.concatenate(
        [dot(normed[...], query_own[...]), dot(normed[...], query_oth[:, 2 * width:])], 1
    ).astype(BF16)
    is_own = (section + j) % 2 == core
    column = lax.broadcasted_iota(jnp.int32, (FR, MEMF), 1)
    scores, values = [], []
    for k, chip in enumerate(CHIPS):
        utt = (section + 2 * (slot ^ chip) + j) % MB
        place = (utt ^ me) >> 1 if ring else utt >> 1
        here = pl.ds(pl.multiple_of(place * MEMF, MEMF), MEMF)
        mine, other = kv_own[here, :], kv_oth[here, :]
        other = jnp.concatenate(
            [other[:, n * width:(n + 1) * width] for n in (1, 0, 3, 2)], 1
        )
        kv = jnp.where(is_own, mine, other)
        length = mem_len[utt]
        values.append(kv[:, 2 * width:])
        for h in range(heads):
            found = lax.dot_general(
                queries[k * FR:(k + 1) * FR, h * HD:(h + 1) * HD],
                kv[:, h * HD:(h + 1) * HD],
                (((1,), (1,)), ((), ())),
                preferred_element_type=F32,
            )
            found = found * (1.0 / math.sqrt(HD))
            scores.append(jnp.where(column < length, found, -jnp.inf))
    score = jnp.concatenate(scores, 0)
    expo = jnp.exp(score - jnp.max(score, -1, keepdims=True))
    probs = (expo / jnp.sum(expo, -1, keepdims=True)).astype(BF16)
    for k in range(4):
        for h in range(heads):
            at = (k * heads + h) * FR
            outs[k // 2][k % 2 * FR:(k % 2 + 1) * FR, h * HD:(h + 1) * HD] = dot(
                probs[at:at + FR], values[k][:, h * HD:(h + 1) * HD]
            ).astype(BF16)


def attend(j, ring, mem_len, pieces, weights, kv):
    depth, width = weights[0].shape
    return pl.pallas_call(
        functools.partial(attend_kernel, j, ring),
        out_shape=[jax.ShapeDtypeStruct((2 * FR, 2 * width), BF16)] * 2,
        in_specs=[pl.BlockSpec(memory_space=pltpu.SMEM)] + whole(8),
        out_specs=whole(2),
        scratch_shapes=[pltpu.VMEM((4 * FR, depth), BF16)],
        compiler_params=pltpu.CompilerParams(vmem_limit_bytes=VMEM_BYTES),
        cost_estimate=pl.CostEstimate(flops=0, bytes_accessed=0, transcendentals=0),
    )(mem_len, *pieces, *weights, *kv)


def project_kernel(near, skip, place, tok_len, *refs):
    refs = refs[skip:]
    att, weights, x_refs, out = refs[:8], refs[8:-3], refs[-3:-1], refs[-1]
    me = lax.axis_index("section")
    slot = (me % GROUP) ^ (NEAR if near else 0)
    first_row = (me // GROUP) * MB + 2 * slot
    width = att[0].shape[1] // 2
    columns = []
    for n in range(2):
        for k in range(4):
            at = FR if near != (k % 2 == 1) else 0
            columns.append(jnp.concatenate(
                [att[j * 4 + k][at:at + FR, n * width:(n + 1) * width] for j in range(2)], 0
            ))
    total, done = None, 0
    for weight in weights:
        count = weight.shape[0] // width
        term = dot(jnp.concatenate(columns[done:done + count], 1), weight[...])
        total = term if total is None else total + term
        done += count
    row = lax.broadcasted_iota(jnp.int32, (FR, total.shape[1]), 0)
    for j, x_ref in enumerate(x_refs):
        branch = jnp.where(row < tok_len[first_row + j], total[j * FR:(j + 1) * FR], 0.0)
        out[j * FR:(j + 1) * FR, :] = (x_ref[...].astype(F32) + branch).astype(BF16)


def project(near, place, tok_len, att, own, oth, pieces, x_first, x_last, into=None):
    width, depth = own.shape
    rows = 2 * FR
    tile = 512
    cols = pieces[0][0][0].shape[1]
    steps = cols // tile

    def everywhere(i, place):
        return 0, place[0] * steps + i

    def here(i, place):
        return 0, i

    att_specs = [pl.BlockSpec((2 * FR, 2 * width), lambda i, place: (0, 0))] * 8
    weights, weight_specs = [], []
    into = [] if near or into is None else [into]
    for mine, others in zip((own, oth), pieces):
        weights.append(mine)
        weight_specs.append(pl.BlockSpec((width, tile), everywhere))
        for n, (array, block) in enumerate(others):
            height = array.shape[0] if n else width
            weights.append(array)
            weight_specs.append(
                pl.BlockSpec((height, tile), lambda i, place, block=block: (block, i))
            )
    x_specs = [
        pl.BlockSpec((FR, tile), lambda i, place, at=ref.shape[0] // FR - 1: (at, everywhere(i, place)[1]))
        for ref in (x_first, x_last)
    ]
    return pl.pallas_call(
        functools.partial(project_kernel, near, len(into)),
        out_shape=jax.ShapeDtypeStruct((rows, cols if near else depth), BF16),
        grid_spec=pltpu.PrefetchScalarGridSpec(
            num_scalar_prefetch=1,
            grid=(steps,),
            in_specs=[pl.BlockSpec(memory_space=pltpu.SMEM)] + [pl.BlockSpec(memory_space=pl.ANY)] * len(into) + att_specs + weight_specs + x_specs,
            out_specs=pl.BlockSpec((rows, tile), here if near else everywhere),
        ),
        compiler_params=pltpu.CompilerParams(
            vmem_limit_bytes=WIDE_VMEM_BYTES, dimension_semantics=("arbitrary",)
        ),
        cost_estimate=pl.CostEstimate(flops=0, bytes_accessed=0, transcendentals=0),
        input_output_aliases={2: 0} if into else {},
    )(place, tok_len, *into, *att, *weights, x_first, x_last)


def assemble_kernel(place, mine, theirs_a, theirs_b, out):
    for k, ref in enumerate((theirs_a, theirs_b)):
        @pl.when(pl.program_id(0) == k)
        def _(ref=ref):
            out[...] = ref[...]


def assemble(place, mine, theirs):
    rows, cols = theirs[0].shape
    return pl.pallas_call(
        assemble_kernel,
        out_shape=jax.ShapeDtypeStruct(mine.shape, BF16),
        grid_spec=pltpu.PrefetchScalarGridSpec(
            num_scalar_prefetch=1,
            grid=(2,),
            in_specs=[pl.BlockSpec(memory_space=pl.ANY)]
            + [pl.BlockSpec((rows, cols), lambda i, place: (0, 0))] * 2,
            out_specs=pl.BlockSpec((rows, cols), lambda i, place: (0, place[i])),
        ),
        input_output_aliases={1: 0},
        compiler_params=pltpu.CompilerParams(vmem_limit_bytes=VMEM_BYTES),
    )(place, mine, *theirs)


def shards(arriving, memory, w_query, w_key, w_value, w_out, tok_len, mem_len):
    me = lax.axis_index("section")
    size = lax.axis_size("section")
    group = lax.axis_index("groups")
    side = (me // NEAR) % 2
    depth = arriving.shape[1]
    ring = size == MB and memory.shape[0] == MEMF

    part_cols = depth // 4
    to_near = lax.dynamic_slice_in_dim(w_out, (2 * (1 - side) + group) * part_cols, part_cols, 1)
    to_far = lax.dynamic_slice_in_dim(w_out, (2 * side + group) * part_cols, part_cols, 1)
    if not ring:
        gathered = lax.all_gather(memory, "section", axis=0, tiled=True)
        gathered = gathered.reshape(MB // 2, 2, MEMF, depth)
        gathered = lax.dynamic_index_in_dim(gathered, me & 1, 1, keepdims=False)
        gathered = [gathered[k] for k in range(MB // 2)]

    out_near = flip(to_near, NEAR)
    out_core = flip(w_out, CORE)
    kv_pair = jnp.concatenate([w_key, w_value, w_query], 1)
    if ring:
        mem_hop, mem_near, mem_far = hop(memory), flip(memory, NEAR), flip(memory, FAR)
    else:
        mem_hop = mem_near = mem_far = out_near
    mem_hop, mem_near, mem_far, out_near, out_core, arriving, kv_pair = together(
        mem_hop, mem_near, mem_far, out_near, out_core, arriving, kv_pair
    )
    first_hop = hop(arriving[:FR])
    kv_pair = flip(kv_pair, CORE)
    if ring:
        hop_far, hop_near, mem_diag = flip(mem_hop, FAR), flip(mem_hop, NEAR), flip(mem_far, NEAR)
    else:
        hop_far = hop_near = mem_diag = mem_far
    first_hop, hop_far, hop_near, mem_diag, kv_pair, arriving, out_near = together(
        first_hop, hop_far, hop_near, mem_diag, kv_pair, arriving, out_near
    )
    kv_weights = [w_key, w_value, kv_pair]
    last_hop = hop(arriving[FR:])
    first_far, first_near = flip(first_hop, FAR), flip(first_hop, NEAR)
    hop_diag = flip(hop_far, NEAR) if ring else hop_far
    cross_near = across(out_near)
    mem_first = [memory, mem_near, mem_far, mem_diag] if ring else gathered[:4]
    kv_first = keys_values(mem_first, kv_weights)
    last_hop, first_far, first_near, hop_diag, cross_near, kv_first, to_far = together(
        last_hop, first_far, first_near, hop_diag, cross_near, kv_first, to_far
    )
    last_far, last_near, first_diag = flip(last_hop, FAR), flip(last_hop, NEAR), flip(first_far, NEAR)
    out_far = flip(to_far, FAR)
    near_core = flip(jnp.concatenate([out_near, cross_near], 0), CORE)
    mem_second = [mem_hop, hop_near, hop_far, hop_diag] if ring else gathered[4:]
    kv_second = keys_values(mem_second, kv_weights, kv_first)
    last_far, last_near, first_diag, out_far, near_core, kv_second, out_near = together(
        last_far, last_near, first_diag, out_far, near_core, kv_second, out_near
    )
    query_pair = [w_query, kv_pair]
    last_diag = flip(last_far, NEAR)
    out_diag = flip(out_near, FAR)
    cross_far = across(out_far)
    kv = [kv_second, flip(kv_second, CORE)]
    first = [first_hop, first_near, first_far, first_diag]
    here, there = attend(0, ring, mem_len, first, query_pair, kv)
    att = [here, flip(here, NEAR), flip(there, FAR), flip(there, NEAR | FAR)]
    last_diag, out_diag, cross_far, *att[1:3] = together(
        last_diag, out_diag, cross_far, *att[1:3]
    )
    cross_diag = across(out_diag)
    last = [last_hop, last_near, last_far, last_diag]
    here, there = attend(1, ring, mem_len, last, query_pair, kv)
    att += [here, flip(here, NEAR), flip(there, FAR), flip(there, NEAR | FAR)]
    fetched = jnp.concatenate([out_far, out_diag], 0)
    fetched, cross_far, cross_diag = together(fetched, cross_far, cross_diag, att[3], *att[5:])[:3]
    handed = [cross_far, cross_diag]
    handed_core = [flip(part, CORE) for part in handed]
    fetched_core = flip(after(fetched, *handed_core), CORE)
    fetched = [[(out_near, 0), (fetched, 0)], [(near_core, 0), (fetched_core, 0)]]
    handed = [
        [(cross_near, 0)] + [(part, 0) for part in handed],
        [(near_core, 1)] + [(part, 0) for part in handed_core],
    ]
    quarters = jnp.stack(
        [2 * side + group, 2 * side + 1 - group, 2 - 2 * side + group, 3 - 2 * side - group]
    ).astype(jnp.int32)
    def part(near, n, pieces, into=None):
        at = 1 if near else 0
        return project(
            near, quarters[n:n + 1], tok_len, att, w_out, out_core, pieces, first[at], last[at], into
        )

    theirs_b = flip(part(True, 1, handed), NEAR)
    theirs_a = flip(part(True, 0, fetched), NEAR)
    mine = part(False, 1, handed, part(False, 0, fetched))
    return assemble(quarters[2:], mine, [theirs_a, theirs_b])


def solution(mesh):
    return jax.shard_map(
        shards,
        mesh=mesh,
        in_specs=(
            P(("groups", "section"), None),
            P(("groups", "section"), None),
            P(None, "section"),
            P(None, "section"),
            P(None, "section"),
            P("section", None),
            P("groups"),
            P("groups"),
        ),
        out_specs=P(("groups", "section"), None),
        check_vma=False,
    )
```

```python
import functools
import math

import jax
import jax.numpy as jnp
from jax import lax
from jax.experimental import pallas as pl
from jax.experimental.pallas import tpu as pltpu
from jax.sharding import PartitionSpec as P

HD = 128
FR = 64
GROUP = 8
MB = 16
MEMF = 64
NORM_EPS = 1e-06
BF16 = jnp.bfloat16
F32 = jnp.float32
VMEM_BYTES = 32 * 2**20
WIDE_VMEM_BYTES = 52 * 2**20

CORE, NEAR, FAR = 1, 2, 4
CHIPS = (0, NEAR, FAR, NEAR | FAR)


def flip(value, bits):
    size = lax.axis_size("section")
    return lax.ppermute(value, "section", [(i, i ^ bits) for i in range(size)])


def hop(value):
    size = lax.axis_size("section")
    return lax.ppermute(value, "section", [(i, (i + GROUP) % size) for i in range(size)])


def after(value, *others):
    return lax.optimization_barrier((value, *others))[0]


def together(*values):
    return lax.optimization_barrier(values)


def across(value):
    return lax.ppermute(value, "groups", [(0, 1), (1, 0)])


def whole(count):
    return [pl.BlockSpec(memory_space=pltpu.VMEM)] * count


def dot(a, b):
    return jnp.dot(a, b, preferred_element_type=F32)


def keys_values_kernel(*refs):
    *mem_refs, key_own, val_own, pair_oth = refs[:7]
    earlier, out, rows = refs[7:-2], refs[-2], refs[-1]
    done = earlier[0].shape[0] if earlier else 0
    if earlier:
        out[:done, :] = earlier[0][...]
    for k, ref in enumerate(mem_refs):
        rows[k * MEMF:(k + 1) * MEMF, :] = ref[:MEMF]
    width = key_own.shape[1]
    weights = (key_own[...], pair_oth[:, :width], val_own[...], pair_oth[:, width:2 * width])
    for k, weight in enumerate(weights):
        out[done:, k * width:(k + 1) * width] = dot(rows[...], weight).astype(BF16)


def keys_values(pieces, weights, *earlier):
    depth, width = weights[0].shape
    rows = len(pieces) * MEMF
    total = rows + sum(part.shape[0] for part in earlier)
    return pl.pallas_call(
        keys_values_kernel,
        out_shape=jax.ShapeDtypeStruct((total, 4 * width), BF16),
        in_specs=whole(len(pieces) + 3 + len(earlier)),
        out_specs=pl.BlockSpec(memory_space=pltpu.VMEM),
        scratch_shapes=[pltpu.VMEM((rows, depth), BF16)],
        compiler_params=pltpu.CompilerParams(vmem_limit_bytes=VMEM_BYTES),
        cost_estimate=pl.CostEstimate(flops=0, bytes_accessed=0, transcendentals=0),
    )(*pieces, *weights, *earlier)


def attend_kernel(j, ring, *refs):
    mem_len, x0, x1, x2, x3, query_own, query_oth = refs[:7]
    kv_own, kv_oth = refs[7:9]
    earlier, outs, normed = refs[9:-3 - j], refs[-3 - j:-1], refs[-1]
    width = query_own.shape[1]
    heads = 2 * width // HD
    me = lax.axis_index("section")
    section, slot, core = me // GROUP, me % GROUP, me % 2
    for k, ref in enumerate((x0, x1, x2, x3)):
        wide = ref[ref.shape[0] - FR:].astype(F32)
        scale = lax.rsqrt(jnp.mean(wide * wide, -1, keepdims=True) + NORM_EPS)
        normed[k * FR:(k + 1) * FR, :] = (wide * scale).astype(BF16)
    queries = jnp.concatenate(
        [dot(normed[...], query_own[...]), dot(normed[...], query_oth[:, 2 * width:])], 1
    ).astype(BF16)
    is_own = (section + j) % 2 == core
    column = lax.broadcasted_iota(jnp.int32, (FR, MEMF), 1)
    scores, values = [], []
    for k, chip in enumerate(CHIPS):
        utt = (section + 2 * (slot ^ chip) + j) % MB
        place = (utt ^ me) >> 1 if ring else utt >> 1
        here = pl.ds(pl.multiple_of(place * MEMF, MEMF), MEMF)
        mine, other = kv_own[here, :], kv_oth[here, :]
        other = jnp.concatenate(
            [other[:, n * width:(n + 1) * width] for n in (1, 0, 3, 2)], 1
        )
        kv = jnp.where(is_own, mine, other)
        length = mem_len[utt]
        values.append(kv[:, 2 * width:])
        for h in range(heads):
            found = lax.dot_general(
                queries[k * FR:(k + 1) * FR, h * HD:(h + 1) * HD],
                kv[:, h * HD:(h + 1) * HD],
                (((1,), (1,)), ((), ())),
                preferred_element_type=F32,
            )
            found = found * (1.0 / math.sqrt(HD))
            scores.append(jnp.where(column < length, found, -jnp.inf))
    score = jnp.concatenate(scores, 0)
    expo = jnp.exp(score - jnp.max(score, -1, keepdims=True))
    probs = (expo / jnp.sum(expo, -1, keepdims=True)).astype(BF16)
    for k in range(4):
        for h in range(heads):
            at = (k * heads + h) * FR
            outs[k // 2][k % 2 * FR:(k % 2 + 1) * FR, h * HD:(h + 1) * HD] = dot(
                probs[at:at + FR], values[k][:, h * HD:(h + 1) * HD]
            ).astype(BF16)
    if earlier:
        outs[2][:2 * FR, :] = earlier[0][...]
        outs[2][2 * FR:, :] = outs[1][...]


def attend(j, ring, mem_len, pieces, weights, kv, *earlier):
    depth, width = weights[0].shape
    heights = [2 * FR] * 2 + [4 * FR] * len(earlier)
    return pl.pallas_call(
        functools.partial(attend_kernel, j, ring),
        out_shape=[jax.ShapeDtypeStruct((height, 2 * width), BF16) for height in heights],
        in_specs=[pl.BlockSpec(memory_space=pltpu.SMEM)] + whole(8 + len(earlier)),
        out_specs=whole(len(heights)),
        scratch_shapes=[pltpu.VMEM((4 * FR, depth), BF16)],
        compiler_params=pltpu.CompilerParams(vmem_limit_bytes=VMEM_BYTES),
        cost_estimate=pl.CostEstimate(flops=0, bytes_accessed=0, transcendentals=0),
    )(mem_len, *pieces, *weights, *kv, *earlier)


def project_kernel(near, skip, place, tok_len, *refs):
    refs = refs[skip:]
    att, weights, x_refs, out = refs[:8], refs[8:-3], refs[-3:-1], refs[-1]
    me = lax.axis_index("section")
    slot = (me % GROUP) ^ (NEAR if near else 0)
    first_row = (me // GROUP) * MB + 2 * slot
    width = att[0].shape[1] // 2
    columns = []
    for n in range(2):
        for k in range(4):
            at = FR if near != (k % 2 == 1) else 0
            columns.append(jnp.concatenate(
                [att[j * 4 + k][at:at + FR, n * width:(n + 1) * width] for j in range(2)], 0
            ))
    total, done = None, 0
    for weight in weights:
        count = weight.shape[0] // width
        term = dot(jnp.concatenate(columns[done:done + count], 1), weight[...])
        total = term if total is None else total + term
        done += count
    row = lax.broadcasted_iota(jnp.int32, (FR, total.shape[1]), 0)
    for j, x_ref in enumerate(x_refs):
        branch = jnp.where(row < tok_len[first_row + j], total[j * FR:(j + 1) * FR], 0.0)
        out[j * FR:(j + 1) * FR, :] = (x_ref[...].astype(F32) + branch).astype(BF16)


def project(near, place, tok_len, att, own, oth, pieces, x_first, x_last, into=None):
    width, depth = own.shape
    rows = 2 * FR
    tile = 512
    cols = pieces[0][0][0].shape[1]
    steps = cols // tile

    def everywhere(i, place):
        return 0, place[0] * steps + i

    def here(i, place):
        return 0, i

    att_specs = [
        pl.BlockSpec((2 * FR, 2 * width), lambda i, place, block=block: (block, 0)) for _, block in att
    ]
    att = [array for array, _ in att]
    weights, weight_specs = [], []
    into = [] if near or into is None else [into]
    for mine, others in zip((own, oth), pieces):
        weights.append(mine)
        weight_specs.append(pl.BlockSpec((width, tile), everywhere))
        for n, (array, block) in enumerate(others):
            height = array.shape[0] if n else width
            weights.append(array)
            weight_specs.append(
                pl.BlockSpec((height, tile), lambda i, place, block=block: (block, i))
            )
    x_specs = [
        pl.BlockSpec((FR, tile), lambda i, place, at=ref.shape[0] // FR - 1: (at, everywhere(i, place)[1]))
        for ref in (x_first, x_last)
    ]
    return pl.pallas_call(
        functools.partial(project_kernel, near, len(into)),
        out_shape=jax.ShapeDtypeStruct((rows, cols if near else depth), BF16),
        grid_spec=pltpu.PrefetchScalarGridSpec(
            num_scalar_prefetch=1,
            grid=(steps,),
            in_specs=[pl.BlockSpec(memory_space=pltpu.SMEM)] + [pl.BlockSpec(memory_space=pl.ANY)] * len(into) + att_specs + weight_specs + x_specs,
            out_specs=pl.BlockSpec((rows, tile), here if near else everywhere),
        ),
        compiler_params=pltpu.CompilerParams(
            vmem_limit_bytes=WIDE_VMEM_BYTES, dimension_semantics=("arbitrary",)
        ),
        cost_estimate=pl.CostEstimate(flops=0, bytes_accessed=0, transcendentals=0),
        input_output_aliases={2: 0} if into else {},
    )(place, tok_len, *into, *att, *weights, x_first, x_last)


def assemble_kernel(place, mine, theirs_a, theirs_b, out):
    for k, ref in enumerate((theirs_a, theirs_b)):
        @pl.when(pl.program_id(0) == k)
        def _(ref=ref):
            out[...] = ref[...]


def assemble(place, mine, theirs):
    rows, cols = theirs[0].shape
    return pl.pallas_call(
        assemble_kernel,
        out_shape=jax.ShapeDtypeStruct(mine.shape, BF16),
        grid_spec=pltpu.PrefetchScalarGridSpec(
            num_scalar_prefetch=1,
            grid=(2,),
            in_specs=[pl.BlockSpec(memory_space=pl.ANY)]
            + [pl.BlockSpec((rows, cols), lambda i, place: (0, 0))] * 2,
            out_specs=pl.BlockSpec((rows, cols), lambda i, place: (0, place[i])),
        ),
        input_output_aliases={1: 0},
        compiler_params=pltpu.CompilerParams(vmem_limit_bytes=VMEM_BYTES),
    )(place, mine, *theirs)


def shards(arriving, memory, w_query, w_key, w_value, w_out, tok_len, mem_len):
    me = lax.axis_index("section")
    size = lax.axis_size("section")
    group = lax.axis_index("groups")
    side = (me // NEAR) % 2
    depth = arriving.shape[1]
    ring = size == MB and memory.shape[0] == MEMF

    part_cols = depth // 4
    to_near = lax.dynamic_slice_in_dim(w_out, (2 * (1 - side) + group) * part_cols, part_cols, 1)
    to_far = lax.dynamic_slice_in_dim(w_out, (2 * side + group) * part_cols, part_cols, 1)
    if not ring:
        gathered = lax.all_gather(memory, "section", axis=0, tiled=True)
        gathered = gathered.reshape(MB // 2, 2, MEMF, depth)
        gathered = lax.dynamic_index_in_dim(gathered, me & 1, 1, keepdims=False)
        gathered = [gathered[k] for k in range(MB // 2)]

    out_near = flip(to_near, NEAR)
    out_core = flip(w_out, CORE)
    kv_pair = jnp.concatenate([w_key, w_value, w_query], 1)
    if ring:
        mem_hop, mem_near, mem_far = hop(memory), flip(memory, NEAR), flip(memory, FAR)
    else:
        mem_hop = mem_near = mem_far = out_near
    mem_hop, mem_near, mem_far, out_near, out_core, arriving, kv_pair = together(
        mem_hop, mem_near, mem_far, out_near, out_core, arriving, kv_pair
    )
    first_hop = hop(arriving[:FR])
    kv_pair = flip(kv_pair, CORE)
    if ring:
        hop_far, hop_near, mem_diag = flip(mem_hop, FAR), flip(mem_hop, NEAR), flip(mem_far, NEAR)
    else:
        hop_far = hop_near = mem_diag = mem_far
    first_hop, hop_far, hop_near, mem_diag, kv_pair, arriving, out_near = together(
        first_hop, hop_far, hop_near, mem_diag, kv_pair, arriving, out_near
    )
    kv_weights = [w_key, w_value, kv_pair]
    last_hop = hop(arriving[FR:])
    first_far, first_near = flip(first_hop, FAR), flip(first_hop, NEAR)
    hop_diag = flip(hop_far, NEAR) if ring else hop_far
    cross_near = across(out_near)
    mem_first = [memory, mem_near, mem_far, mem_diag] if ring else gathered[:4]
    kv_first = keys_values(mem_first, kv_weights)
    last_hop, first_far, first_near, hop_diag, cross_near, kv_first, to_far = together(
        last_hop, first_far, first_near, hop_diag, cross_near, kv_first, to_far
    )
    last_far, last_near, first_diag = flip(last_hop, FAR), flip(last_hop, NEAR), flip(first_far, NEAR)
    out_far = flip(to_far, FAR)
    near_core = flip(jnp.concatenate([out_near, cross_near], 0), CORE)
    mem_second = [mem_hop, hop_near, hop_far, hop_diag] if ring else gathered[4:]
    kv_second = keys_values(mem_second, kv_weights, kv_first)
    last_far, last_near, first_diag, out_far, near_core, kv_second, out_near = together(
        last_far, last_near, first_diag, out_far, near_core, kv_second, out_near
    )
    query_pair = [w_query, kv_pair]
    last_diag = flip(last_far, NEAR)
    out_diag = flip(out_near, FAR)
    cross_far = across(out_far)
    kv = [kv_second, flip(kv_second, CORE)]
    first = [first_hop, first_near, first_far, first_diag]
    here, there = attend(0, ring, mem_len, first, query_pair, kv)
    att = [here, flip(here, NEAR), flip(there, FAR)]
    last_diag, out_diag, cross_far, *att[1:3] = together(
        last_diag, out_diag, cross_far, *att[1:3]
    )
    cross_diag = across(out_diag)
    last = [last_hop, last_near, last_far, last_diag]
    here, there, both = attend(1, ring, mem_len, last, query_pair, kv, there)
    att += [here, flip(here, NEAR), flip(there, FAR), flip(both, NEAR | FAR)]
    fetched = jnp.concatenate([out_far, out_diag], 0)
    fetched, cross_diag = together(fetched, cross_diag, *att[4:])[:2]
    handed = [cross_far, cross_diag]
    handed_core = [flip(part, CORE) for part in handed]
    fetched_core = flip(after(fetched, *handed_core), CORE)
    fetched = [[(out_near, 0), (fetched, 0)], [(near_core, 0), (fetched_core, 0)]]
    handed = [
        [(cross_near, 0)] + [(part, 0) for part in handed],
        [(near_core, 1)] + [(part, 0) for part in handed_core],
    ]
    quarters = jnp.stack(
        [2 * side + group, 2 * side + 1 - group, 2 - 2 * side + group, 3 - 2 * side - group]
    ).astype(jnp.int32)
    att = [(att[k], 0) for k in (0, 1, 2, 6, 3, 4, 5)] + [(att[6], 1)]

    def part(near, n, pieces, into=None):
        at = 1 if near else 0
        return project(
            near, quarters[n:n + 1], tok_len, att, w_out, out_core, pieces, first[at], last[at], into
        )

    theirs_b = flip(part(True, 1, handed), NEAR)
    theirs_a = flip(part(True, 0, fetched), NEAR)
    mine = part(False, 1, handed, part(False, 0, fetched))
    return assemble(quarters[2:], mine, [theirs_a, theirs_b])


def solution(mesh):
    return jax.shard_map(
        shards,
        mesh=mesh,
        in_specs=(
            P(("groups", "section"), None),
            P(("groups", "section"), None),
            P(None, "section"),
            P(None, "section"),
            P(None, "section"),
            P("section", None),
            P("groups"),
            P("groups"),
        ),
        out_specs=P(("groups", "section"), None),
        check_vma=False,
    )
```
